128 devices in a mesh: pipe: 8 (over x, core), expert: 16 (over z, y).
Axes of the slice: x: 4, y: 4, z: 4, core: 2. Of those that a mesh axis runs over, the one named last changes fastest.
Arguments:
- tokens: bfloat16 [16384, 7168], P(('pipe', 'expert')), may hold values from -6 to 6
- cotangent: bfloat16 [16384, 7168], P(('pipe', 'expert')), may hold values from -6 to 6
- expert_ids: int32 [16384, 8], P(('pipe', 'expert')), may hold values from 0 to 255, as said below
- gate_probs: bfloat16 [16384, 8], P(('pipe', 'expert')), may hold values from 0.049804688 to 1
- w_gate: bfloat16 [16, 7168, 2048], P('expert', None, 'pipe'), may hold values from -0.0625 to 0.0625
- w_up: bfloat16 [16, 7168, 2048], P('expert', None, 'pipe'), may hold values from -0.0625 to 0.0625
- w_down: bfloat16 [16, 2048, 7168], P('expert', 'pipe'), may hold values from -0.125 to 0.125
Outputs:
- grad_gate_w: bfloat16 [16, 7168, 2048], P('expert', None, 'pipe')
- grad_up_w: bfloat16 [16, 7168, 2048], P('expert', None, 'pipe')
- grad_down_w: bfloat16 [16, 2048, 7168], P('expert', 'pipe')
- gate_grad: float32 [16384, 8], P(('pipe', 'expert'))
The draws below stay inside these ranges and needn't reach their ends.
Inputs may be any that keep to these rules, and one draw needn't show every extreme that they name: `expert_ids`: each token's 8 ids are distinct and its k-th id lies in group k, that is among k * 32 to (k + 1) * 32 - 1. The tokens of one device (aligned blocks of 128 rows) name any expert of the window at most 8 times, and one expert of the window is named exactly 8 times in every block.
All inputs are finite; a program needn't handle non-finite values.
Results may differ from the reference program's by a relative error of at most 0.011.
Values may be sent and summed in bfloat16 or wider, within the bound.
No kernel may reach another device: no remote copies, remote signals or barrier semaphores. Data moves between devices by JAX's collectives and lax.ppermute only.
A program may use at most 192 MiB of HBM per device.

```python
import math
import jax
import jax.numpy as jnp
from jax import lax

D = 7168
HID = 2048
TOP = 8
GROUPS = 8
TOK_DEV = 128
CAP = 8
WIN = 16
GROUP_SIZE = 32
TOKENS = 16384
ROWS = 1024
N_PIPE = 8
N_EXPERT = 16


def draw_expert_ids(key, part):
    key = jax.random.fold_in(key, 11)
    key_hot, key_count, key_order, key_rest = jax.random.split(key, 4)
    sources = N_PIPE * N_EXPERT
    per_group = WIN // GROUPS
    hotness = jax.random.permutation(key_hot, WIN)
    lowest = jnp.where(hotness == 0, CAP, jnp.where(hotness == 1, CAP // 2, 0)).astype(jnp.int32)
    highest = jnp.where(hotness == 0, CAP, jnp.where(hotness == 1, CAP, CAP // 2)).astype(jnp.int32)
    counts = jax.random.randint(key_count, (sources, WIN), lowest[None, :], highest[None, :] + 1)
    lane_counts = counts.reshape(sources, per_group, GROUPS).transpose(0, 2, 1)
    bounds = jnp.cumsum(lane_counts, axis=2)
    scores = jax.random.randint(key_order, (sources, GROUPS, TOK_DEV), 0, 1 << 16) * TOK_DEV
    scores = scores + jnp.arange(TOK_DEV, dtype=jnp.int32)[None, None, :]
    ordering = jnp.argsort(scores, axis=2)
    position = jnp.argsort(ordering, axis=2)
    chosen = jnp.sum((position[:, :, :, None] >= bounds[:, :, None, :]).astype(jnp.int32), axis=3)
    leftover = jax.random.randint(key_rest, (sources, GROUPS, TOK_DEV), per_group, GROUP_SIZE)
    within = jnp.where(chosen < per_group, chosen, leftover)
    routed = jnp.arange(GROUPS, dtype=jnp.int32)[None, :, None] * GROUP_SIZE + within
    return routed.transpose(0, 2, 1).reshape(sources * TOK_DEV, GROUPS).astype(jnp.int32)


def block_scale(own_key, extent, shards, least, high):
    def one(axis_at, blocks):
        heights = jax.random.uniform(jax.random.fold_in(jax.random.fold_in(own_key, 6), axis_at), (blocks,), jnp.float32, least / len(shards), high / len(shards))
        return jnp.repeat(jnp.exp(heights), extent[axis_at] // blocks).reshape((-1,) + (1,) * (len(extent) - axis_at - 1))

    level = one(*shards[0])
    for cut in shards[1:]:
        level = level * one(*cut)
    return level


def scatter_about(own_key, dims, deviation, reach, cuts=(), kind=jnp.bfloat16):
    loudness = block_scale(own_key, dims, cuts, -0.22, 0.18) if cuts else 1.0
    array = jax.random.normal(own_key, dims, jnp.float32) * deviation * loudness
    return jnp.minimum(jnp.maximum(array, -reach), reach).astype(kind)


def setup_inputs(seed: int = 0) -> dict:
    streams_of = jax.random.split(jax.random.key(seed), 8)
    return {
        "tokens": scatter_about(streams_of[0], (TOKENS, D), 1.0, 6.0, ((0, 128),)),
        "cotangent": scatter_about(streams_of[1], (TOKENS, D), 1.0, 6.0, ((0, 128),)),
        "expert_ids": draw_expert_ids(jax.random.fold_in(streams_of[7], 71), 0),
        "gate_probs": jnp.clip(jnp.exp(math.log(1.0) - 2.9996462 * jax.random.uniform(streams_of[3], (TOKENS, TOP), jnp.float32) ** block_scale(streams_of[3], (TOKENS, TOP), ((0, 128),), -0.2, 0.2)), 0.049804688, 1.0).astype(jnp.bfloat16),
        "w_gate": scatter_about(streams_of[4], (WIN, D, HID), D ** -0.5, 0.0625, ((0, 16), (2, 8))),
        "w_up": scatter_about(streams_of[5], (WIN, D, HID), D ** -0.5, 0.0625, ((0, 16), (2, 8))),
        "w_down": scatter_about(streams_of[6], (WIN, HID, D), HID ** -0.5, 0.125, ((0, 16), (1, 8))),
    }


def window_ids():
    experts = jnp.arange(WIN, dtype=jnp.int32)
    return (experts % GROUPS) * GROUP_SIZE + experts // GROUPS


def expert_terms(rows_x, rows_dy, rows_gate, gate_w, up_w, down_w):
    pre_gate = jnp.dot(rows_x, gate_w, preferred_element_type=jnp.float32)
    pre_up = jnp.dot(rows_x, up_w, preferred_element_type=jnp.float32)
    sigmoid_gate = jax.nn.sigmoid(pre_gate)
    activated = pre_gate * sigmoid_gate
    hidden = (activated * pre_up).astype(jnp.bfloat16)
    gate_col = rows_gate.astype(jnp.float32)[:, None]
    weighted = (gate_col * rows_dy.astype(jnp.float32)).astype(jnp.bfloat16)
    grad_down = jnp.dot(hidden.T, weighted, preferred_element_type=jnp.float32)
    projected = jnp.dot(rows_dy, down_w.T, preferred_element_type=jnp.float32)
    row_gate = jnp.sum(hidden.astype(jnp.float32) * projected, axis=1)
    back_hidden = gate_col * projected
    slope = sigmoid_gate * (1.0 + pre_gate * (1.0 - sigmoid_gate))
    grad_pre_gate = (back_hidden * pre_up * slope).astype(jnp.bfloat16)
    grad_pre_up = (back_hidden * activated).astype(jnp.bfloat16)
    grad_gate = jnp.dot(rows_x.T, grad_pre_gate, preferred_element_type=jnp.float32)
    grad_up = jnp.dot(rows_x.T, grad_pre_up, preferred_element_type=jnp.float32)
    return grad_gate, grad_up, grad_down, row_gate


def reference(tokens, cotangent, expert_ids, gate_probs, w_gate, w_up, w_down):
    routed = window_ids()
    matches = expert_ids[:, :, None] == routed[None, None, :]
    routed_here = jnp.any(matches, axis=1).astype(jnp.int32)
    per_device = routed_here.reshape(N_PIPE * N_EXPERT, TOK_DEV, WIN)
    slot_rank = (jnp.cumsum(per_device, axis=1) - per_device).reshape(TOKENS, WIN)
    device_of = (jnp.arange(TOKENS, dtype=jnp.int32) // TOK_DEV)[:, None]
    row_index = jnp.where(routed_here == 1, device_of * CAP + slot_rank, ROWS).astype(jnp.int32)
    gate_sel = jnp.sum(jnp.where(matches, gate_probs.astype(jnp.float32)[:, :, None], 0.0), axis=1)
    gate_sel = gate_sel.astype(jnp.bfloat16)

    def one_expert(expert):
        rows_at = row_index[:, expert]
        rows_x = jnp.zeros((ROWS, D), jnp.bfloat16).at[rows_at].set(tokens, mode="drop")
        rows_dy = jnp.zeros((ROWS, D), jnp.bfloat16).at[rows_at].set(cotangent, mode="drop")
        rows_gate = jnp.zeros((ROWS,), jnp.bfloat16).at[rows_at].set(gate_sel[:, expert], mode="drop")
        grads = expert_terms(rows_x, rows_dy, rows_gate, w_gate[expert], w_up[expert], w_down[expert])
        return (grads[0].astype(jnp.bfloat16), grads[1].astype(jnp.bfloat16), grads[2].astype(jnp.bfloat16), grads[3])

    grad_gate_w, grad_up_w, grad_down_w, row_gate = lax.map(one_expert, jnp.arange(WIN, dtype=jnp.int32))
    clipped = jnp.minimum(row_index, ROWS - 1).astype(jnp.int32)
    picked = jnp.take_along_axis(row_gate.T, clipped, axis=0)
    picked = jnp.where(routed_here == 1, picked, 0.0)
    gate_grad = jnp.sum(jnp.where(matches, picked[:, None, :], 0.0), axis=2)
    return grad_gate_w, grad_up_w, grad_down_w, gate_grad
```

```python
import jax
import jax.numpy as jnp
from jax import lax
from jax.sharding import Mesh, PartitionSpec as P

GROUPS = 8
CAP = 8
GROUP_SIZE = 32
NX, NC, NZ, NY = 4, 2, 4, 4

X_GROUPS = ((1024,), (2048,), (2048, 2048))
DY_GROUPS = ((2048, 2048), (2048, 1024))


def shift(x, axis, by):
    n = lax.axis_size(axis)
    return lax.ppermute(x, axis, [(i, (i + by) % n) for i in range(n)])


def exchange_yz(tiles):
    over_y = [tiles[:, 0]] + [shift(tiles[:, k], "y", k) for k in range(1, NY)]
    over_z = [jnp.stack([part[k] for part in over_y]) for k in range(NZ)]
    over_z = over_z[:1] + [shift(over_z[k], "z", k) for k in range(1, NZ)]
    return jnp.stack(over_z)


def gather_pipe(block):
    half = block.shape[0] // 2
    from_left = shift(block, "x", 1)
    from_right = shift(block, "x", -1)
    far_low = shift(from_left[:half], "x", 1)
    far_high = shift(from_right[half:], "x", -1)
    mine = jnp.concatenate([block, from_left, from_right, far_low, far_high])
    return jnp.concatenate([mine, shift(mine, "core", 1)])


def return_rows(row_gate):
    parts = row_gate.reshape(NC, NX, NZ, NY, CAP)
    mine = parts[0] + shift(parts[1], "core", 1)
    mine = mine[0] + shift(mine[1], "x", -1) + shift(mine[2], "x", 1) + shift(mine[3], "x", 2)
    back_z = jnp.stack([mine[0]] + [shift(mine[k], "z", -k) for k in range(1, NZ)])
    return jnp.stack([back_z[:, 0]] + [shift(back_z[:, k], "y", -k) for k in range(1, NY)], axis=1)


def per_device(tokens, cotangent, expert_ids, gate_probs, w_gate, w_up, w_down):
    tok_here, features = tokens.shape
    z, y = lax.axis_index("z"), lax.axis_index("y")
    dz = jnp.arange(NZ, dtype=jnp.int32)[:, None]
    dy = jnp.arange(NY, dtype=jnp.int32)[None, :]
    experts = (((z + dz) % NZ) * NY + (y + dy) % NY).reshape(-1)
    columns = experts.shape[0]
    routed = experts % GROUPS * GROUP_SIZE + experts // GROUPS
    matches = expert_ids[:, :, None] == routed[None, None, :]
    routed_here = jnp.any(matches, axis=1).astype(jnp.int32)
    slot_rank = jnp.cumsum(routed_here, axis=0) - routed_here
    slot_hot = jnp.logical_and(
        slot_rank[:, :, None] == jnp.arange(CAP, dtype=jnp.int32)[None, None, :],
        routed_here[:, :, None] == 1,
    )
    gates = gate_probs.astype(jnp.float32)
    gate_sel = jnp.sum(jnp.where(matches, gates[:, :, None], 0.0), axis=1)
    placer = slot_hot.astype(jnp.bfloat16).reshape(tok_here, columns * CAP)
    placer_gate = (
        jnp.where(slot_hot, gate_sel[:, :, None], 0.0).astype(jnp.bfloat16).reshape(tok_here, columns * CAP)
    )
    w_both = jnp.concatenate([w_gate[0], w_up[0]], axis=1)
    down = w_down[0]
    width = w_gate.shape[2]

    def tiles_of(place, source, at, size):
        tiles = lax.dot_general(
            place, source[:, at : at + size], (((0,), (0,)), ((), ())), preferred_element_type=jnp.float32
        )
        return tiles.astype(jnp.bfloat16).reshape(NZ, NY, CAP, size)

    def rows_of(place, source, groups):
        at = 0
        for group in groups:
            block = exchange_yz(tiles_of(place, source, at, sum(group))).reshape(columns * CAP, sum(group))
            start = 0
            for size in group:
                yield at + start, size, gather_pipe(block[:, start : start + size])
                start += size
            at += sum(group)

    pre = jnp.zeros((NX * NC * columns * CAP, 2 * width), jnp.float32)
    x_turned = []
    for at, size, rows in rows_of(placer, tokens, X_GROUPS):
        pre = pre + jnp.dot(rows, w_both[at : at + size], preferred_element_type=jnp.float32)
        x_turned.append(rows.T)
    pre_gate, pre_up = pre[:, :width], pre[:, width:]
    sig = jax.nn.sigmoid(pre_gate)
    activated = pre_gate * sig
    hidden = (activated * pre_up).astype(jnp.bfloat16)
    hidden_turned = hidden.T
    weighted_projected = jnp.zeros((NX * NC * columns * CAP, width), jnp.float32)
    grad_down = []
    for at, size, rows in rows_of(placer_gate, cotangent, DY_GROUPS):
        weighted_projected = weighted_projected + lax.dot_general(
            rows, down[:, at : at + size], (((1,), (1,)), ((), ())), preferred_element_type=jnp.float32
        )
        grad_down.append(jnp.dot(hidden_turned, rows, preferred_element_type=jnp.float32).astype(jnp.bfloat16))
    row_gate = jnp.sum(hidden.astype(jnp.float32) * weighted_projected, axis=1)
    returned = return_rows(row_gate).reshape(columns, CAP)
    slope = sig * (1.0 + pre_gate * (1.0 - sig))
    grad_pre_gate = (weighted_projected * pre_up * slope).astype(jnp.bfloat16)
    grad_pre_up = (weighted_projected * activated).astype(jnp.bfloat16)
    x_turned = jnp.concatenate(x_turned)
    grad_gate = jnp.dot(x_turned, grad_pre_gate, preferred_element_type=jnp.float32)
    grad_up = jnp.dot(x_turned, grad_pre_up, preferred_element_type=jnp.float32)

    slot_values = jnp.sum(jnp.where(slot_hot, returned[None], 0.0), axis=2)
    picked = jnp.sum(jnp.where(matches, slot_values[:, None, :], 0.0), axis=2)
    gate_grad = picked / gates
    return (
        grad_gate.astype(jnp.bfloat16)[None],
        grad_up.astype(jnp.bfloat16)[None],
        jnp.concatenate(grad_down, axis=1)[None],
        gate_grad,
    )


def solution(mesh):
    mesh = Mesh(mesh.devices.reshape(NX, NC, NZ, NY), ("x", "core", "z", "y"))
    tokens = P(("x", "core", "z", "y"), None)
    wide = P(("z", "y"), None, ("x", "core"))
    deep = P(("z", "y"), ("x", "core"), None)
    return jax.shard_map(
        per_device,
        mesh=mesh,
        in_specs=(tokens, tokens, tokens, tokens, wide, wide, deep),
        out_specs=(wide, wide, deep, tokens),
        check_vma=False,
    )
```

```python
import math

import jax
import jax.numpy as jnp
from jax import lax
from jax.experimental import pallas as pl
from jax.experimental.pallas import tpu as pltpu
from jax.sharding import Mesh, PartitionSpec as P

GROUPS = 8
CAP = 8
GROUP_SIZE = 32
NX, NC, NZ, NY = 4, 2, 4, 4

X_RAW, X_REST = 1024, 6144
DY = (5120, 2048)
BLOCK, UP_BLOCK = 2048, 1024
PARAMS = pltpu.CompilerParams(vmem_limit_bytes=58 * 2**20)


def after(x, *others):
    return x if not others else lax.optimization_barrier((x, *others))[0]


def shift(x, axis, by):
    n = lax.axis_size(axis)
    return lax.ppermute(x, axis, [(i, (i + by) % n) for i in range(n)])


def exchange_yz(tiles):
    return lax.all_to_all(tiles, ("z", "y"), 0, 0, tiled=True).reshape(-1, tiles.shape[2])


def hop(x, by):
    pairs = [(i * NC + c, (i + by * (1 - 2 * c)) % NX * NC + c) for i in range(NX) for c in range(NC)]
    return lax.ppermute(x, ("x", "core"), pairs)


def stack_rows(*parts):
    parts = [part if isinstance(part, tuple) else (part, 0, part.shape[1]) for part in parts]
    rows = [part[0].shape[0] for part in parts]
    starts = [sum(rows[:k]) for k in range(len(rows))]

    def kernel(*refs):
        out_ref, held, sems = refs[len(rows) :]
        places = [pl.ds(at, n) for at, n in zip(starts, rows)]
        sources = [ref.at[:, pl.ds(at, size)] for ref, (_, at, size) in zip(refs, parts)]
        reads = [
            pltpu.make_async_copy(source, held.at[place], sems.at[0, k])
            for k, (source, place) in enumerate(zip(sources, places))
        ]
        writes = [
            pltpu.make_async_copy(held.at[place], out_ref.at[place], sems.at[1, k]) for k, place in enumerate(places)
        ]
        for read in reads:
            read.start()
        for read, write in zip(reads, writes):
            read.wait()
            write.start()
        for write in writes:
            write.wait()

    out = jax.ShapeDtypeStruct((sum(rows), parts[0][2]), parts[0][0].dtype)
    return pl.pallas_call(
        kernel,
        in_specs=[pl.BlockSpec(memory_space=pl.ANY)] * len(parts),
        out_specs=pl.BlockSpec(memory_space=pl.ANY),
        out_shape=out,
        scratch_shapes=[pltpu.VMEM(out.shape, out.dtype), pltpu.SemaphoreType.DMA((2, len(parts)))],
        compiler_params=PARAMS,
        cost_estimate=cost(0, out, out),
    )(*[part[0] for part in parts])


def cost(flops, *arrays):
    size = sum(a.size * a.dtype.itemsize for a in arrays)
    return pl.CostEstimate(flops=flops, bytes_accessed=size, transcendentals=0)


ANY = pl.BlockSpec(memory_space=pl.ANY)


def row_specs(parts, block):
    return [pl.BlockSpec((part.shape[0], block), lambda i: (0, i)) for part in parts]


def joined(refs):
    return jnp.concatenate([ref[...] for ref in refs])


def forward(parts, w_gate, w_up, at, pre):
    size, count = parts[0].shape[1], len(parts)
    rows = sum(part.shape[0] for part in parts)
    width = w_gate.shape[2]
    block = math.gcd(BLOCK, size, at)
    first = at // block

    def kernel(*refs):
        out_ref = refs[-1]

        @pl.when(pl.program_id(0) == 0)
        def _():
            out_ref[...] = jnp.zeros_like(out_ref) if pre is None else refs[2 + count][...]

        x = joined(refs[2 : 2 + count])
        for j, w_ref in enumerate(refs[:2]):
            out_ref[:, j * width : (j + 1) * width] += jnp.dot(x, w_ref[0], preferred_element_type=jnp.float32)

    whole = pl.BlockSpec((rows, 2 * width), lambda i: (0, 0))
    out = jax.ShapeDtypeStruct((rows, 2 * width), jnp.float32)
    return pl.pallas_call(
        kernel,
        grid=(size // block,),
        in_specs=[pl.BlockSpec((1, block, width), lambda i: (0, first + i, 0))] * 2
        + row_specs(parts, block)
        + ([] if pre is None else [whole]),
        out_specs=whole,
        out_shape=out,
        compiler_params=PARAMS,
        cost_estimate=cost(4 * rows * size * width, *parts, out, out),
    )(w_gate, w_up, *parts, *(() if pre is None else (pre,)))


def down_terms(parts, w_down, hidden_turned, at):
    size, count = parts[0].shape[1], len(parts)
    rows = sum(part.shape[0] for part in parts)
    _, width, features = w_down.shape
    block = math.gcd(BLOCK, size, at)
    first = at // block

    def kernel(*refs):
        down_ref, hidden_ref = refs[:2]
        projected_ref, grad_ref = refs[-2:]

        @pl.when(pl.program_id(0) == 0)
        def _():
            projected_ref[...] = jnp.zeros_like(projected_ref)

        dy = joined(refs[2 : 2 + count])
        projected_ref[...] += lax.dot_general(
            dy, down_ref[0], (((1,), (1,)), ((), ())), preferred_element_type=jnp.float32
        )
        grad_ref[0] = jnp.dot(hidden_ref[...], dy, preferred_element_type=jnp.float32).astype(jnp.bfloat16)

    whole = pl.BlockSpec((rows, width), lambda i: (0, 0))
    wide = pl.BlockSpec((1, width, block), lambda i: (0, 0, first + i))
    outs = [
        jax.ShapeDtypeStruct((rows, width), jnp.float32),
        jax.ShapeDtypeStruct((1, width, features), jnp.bfloat16),
    ]
    return pl.pallas_call(
        kernel,
        grid=(size // block,),
        in_specs=[wide, pl.BlockSpec((width, rows), lambda i: (0, 0))] + row_specs(parts, block),
        out_specs=[whole, wide],
        out_shape=outs,
        compiler_params=PARAMS,
        cost_estimate=cost(4 * rows * size * width, *parts, outs[0]),
    )(w_down, hidden_turned, *parts)


def down_end(parts, w_down, hidden_turned, pre, at, projected, grad_down):
    size, count = parts[0].shape[1], len(parts)
    rows = sum(part.shape[0] for part in parts)
    _, width, features = w_down.shape
    block = math.gcd(1024, size, at)
    first, steps = at // block, size // block
    strip = 128

    def kernel(*refs):
        down_ref, hidden_ref, pre_ref, before_ref = refs[:4]
        grad_ref, gate_ref, up_ref, row_ref, total = refs[-5:]

        @pl.when(pl.program_id(0) == 0)
        def _():
            total[...] = before_ref[...]

        dy = joined(refs[4 : 4 + count])
        total[...] += lax.dot_general(dy, down_ref[0], (((1,), (1,)), ((), ())), preferred_element_type=jnp.float32)
        grad_ref[0] = jnp.dot(hidden_ref[...], dy, preferred_element_type=jnp.float32).astype(jnp.bfloat16)

        @pl.when(pl.program_id(0) == steps - 1)
        def _():
            def some(k, _):
                at_rows = pl.ds(pl.multiple_of(k * strip, strip), strip)
                projected = total[at_rows]
                pre_gate, pre_up = pre_ref[at_rows, :width], pre_ref[at_rows, width:]
                sig = jax.nn.sigmoid(pre_gate)
                activated = pre_gate * sig
                hidden = (activated * pre_up).astype(jnp.bfloat16)
                slope = sig * (1.0 + pre_gate * (1.0 - sig))
                gate_ref[at_rows] = (projected * pre_up * slope).astype(jnp.bfloat16)
                up_ref[at_rows] = (projected * activated).astype(jnp.bfloat16)
                row_ref[at_rows] = jnp.sum(hidden.astype(jnp.float32) * projected, axis=1, keepdims=True)
                return 0

            lax.fori_loop(0, rows // strip, some, 0)

    def whole(*shape):
        return pl.BlockSpec(shape, lambda i: (0, 0))

    wide = pl.BlockSpec((1, width, block), lambda i: (0, 0, first + i))
    grad = jax.ShapeDtypeStruct((rows, width), jnp.bfloat16)
    return pl.pallas_call(
        kernel,
        grid=(steps,),
        in_specs=[wide, whole(width, rows), whole(rows, 2 * width), whole(rows, width)] + row_specs(parts, block) + [ANY],
        out_specs=[wide, whole(rows, width), whole(rows, width), whole(rows, 1)],
        out_shape=[
            jax.ShapeDtypeStruct((1, width, features), jnp.bfloat16),
            grad,
            grad,
            jax.ShapeDtypeStruct((rows, 1), jnp.float32),
        ],
        scratch_shapes=[pltpu.VMEM((rows, width), jnp.float32)],
        input_output_aliases={4 + count: 0},
        compiler_params=PARAMS,
        cost_estimate=cost(4 * rows * size * width, *parts, pre, projected),
    )(w_down, hidden_turned, pre, projected, *parts, grad_down)


def up_terms(parts, last_parts, grad_pre_gate, grad_pre_up):
    rows, width = grad_pre_gate.shape
    count, size, last = len(parts), parts[0].shape[1], last_parts[0].shape[1]
    block = math.gcd(UP_BLOCK, size, last)
    steps, last_steps = size // block, last // block

    def kernel(*refs):
        out_refs = refs[-2:]

        def write(row_refs):
            x = joined(row_refs)
            for pre_ref, out_ref in zip(refs[:2], out_refs):
                out_ref[0] = lax.dot_general(
                    x, pre_ref[...], (((0,), (0,)), ((), ())), preferred_element_type=jnp.float32
                ).astype(jnp.bfloat16)

        pl.when(pl.program_id(0) < steps)(lambda: write(refs[2 : 2 + count]))
        pl.when(pl.program_id(0) >= steps)(lambda: write(refs[2 + count : -2]))

    out = jax.ShapeDtypeStruct((1, size + last, width), jnp.bfloat16)
    whole = pl.BlockSpec((rows, width), lambda i: (0, 0))
    return pl.pallas_call(
        kernel,
        grid=(steps + last_steps,),
        in_specs=[whole, whole]
        + [pl.BlockSpec((part.shape[0], block), lambda i: (0, jnp.minimum(i, steps - 1))) for part in parts]
        + [pl.BlockSpec((part.shape[0], block), lambda i: (0, jnp.maximum(i - steps, 0))) for part in last_parts],
        out_specs=[pl.BlockSpec((1, block, width), lambda i: (0, i, 0))] * 2,
        out_shape=[out, out],
        compiler_params=PARAMS,
        cost_estimate=cost(4 * rows * size * width, *parts, *last_parts, out),
    )(grad_pre_gate, grad_pre_up, *parts, *last_parts)


def return_rows(row_gate):
    x, core = lax.axis_index("x"), lax.axis_index("core")
    to_x = jnp.arange(NX, dtype=jnp.int32)[:, None]
    to_core = jnp.arange(NC, dtype=jnp.int32)[None, :]
    away = (to_x - x) * (1 - 2 * to_core) % NX
    group = jnp.where(to_core == core, 0, NX) + jnp.where(away == 3, 1, jnp.where(away == 1, 2, jnp.where(away == 2, 3, 0)))
    parts = row_gate.reshape(NC * NX, -1)
    pick = group.reshape(-1, 1) == jnp.arange(NC * NX, dtype=jnp.int32)[None, :]
    parts = jnp.sum(jnp.where(pick[:, :, None], parts[None], 0.0), axis=1)
    got = lax.all_to_all(parts.reshape(NC * NX * NZ * NY, CAP), ("x", "core", "z", "y"), 0, 0, tiled=True)
    return jnp.sum(got.reshape(NC * NX, NZ * NY, CAP), axis=0)


def per_device(tokens, cotangent, expert_ids, gate_probs, w_gate, w_up, w_down):
    tok_here = tokens.shape[0]
    columns = NZ * NY
    experts = jnp.arange(columns, dtype=jnp.int32)
    routed = experts % GROUPS * GROUP_SIZE + experts // GROUPS
    matches = expert_ids[:, :, None] == routed[None, None, :]
    routed_here = jnp.any(matches, axis=1).astype(jnp.int32)
    slot_rank = jnp.cumsum(routed_here, axis=0) - routed_here
    slot_hot = jnp.logical_and(
        slot_rank[:, :, None] == jnp.arange(CAP, dtype=jnp.int32)[None, None, :],
        routed_here[:, :, None] == 1,
    )
    gates = gate_probs.astype(jnp.float32)
    gate_sel = jnp.sum(jnp.where(matches, gates[:, :, None], 0.0), axis=1)
    placer = slot_hot.astype(jnp.bfloat16).reshape(tok_here, columns * CAP)
    placer_gate = (
        jnp.where(slot_hot, gate_sel[:, :, None], 0.0).astype(jnp.bfloat16).reshape(tok_here, columns * CAP)
    )
    width = w_gate.shape[2]

    def hidden_of(pre):
        pre_gate, pre_up = pre[:, :width], pre[:, width:]
        return (pre_gate * jax.nn.sigmoid(pre_gate) * pre_up).astype(jnp.bfloat16)

    def tiles_of(place, source, at, size):
        tiles = lax.dot_general(
            place, source[:, at : at + size], (((0,), (0,)), ((), ())), preferred_element_type=jnp.float32
        )
        return tiles.astype(jnp.bfloat16).reshape(columns, CAP, size)

    def on(block, *ties):
        return hop(after(block, *ties), 1)

    def back(block, *ties):
        return hop(after(block, *ties), -1)

    def swap(part):
        return shift(part, "core", 1)

    features = tokens.shape[1]
    d_at = [sum(DY[:k]) for k in range(len(DY))]

    raw = tiles_of(placer, tokens, X_REST, X_RAW).reshape(-1, X_RAW)
    on_r, back_r = hop(raw, 1), hop(raw, -1)
    x = exchange_yz(after(tiles_of(placer, tokens, 0, X_REST), raw))
    rounds = [part.reshape(columns, CAP, X_RAW) for part in (raw, on_r, back_r, hop(on_r, 1))]
    mixed = jnp.concatenate([*rounds, tiles_of(placer_gate, cotangent, 0, features)], axis=2)

    ties = (x, mixed)
    on_x, back_x = on(x, *ties), back(x, *ties)
    mixed = exchange_yz(after(mixed, *ties))

    ties = (mixed, on_x, back_x)
    d = [mixed[:, NX * X_RAW + at : NX * X_RAW + at + size] for at, size in zip(d_at, DY)]
    again_x, on_0, back_0 = on(on_x, *ties), on(d[0], *ties), back(d[0], *ties)
    raw_rows = stack_rows(*[(mixed, k * X_RAW, X_RAW) for k in range(NX)])
    raw_rows = (raw_rows, swap(raw_rows))
    near_x = stack_rows(after(x, *ties), on_x, back_x)
    other_x = swap(near_x)
    pre = forward(raw_rows, w_gate, w_up, X_REST, None)

    ties = (again_x, on_0, back_0, other_x, pre)
    again_0, on_1, back_1 = on(on_0, *ties), on(d[1], *ties), back(d[1], *ties)
    x_rows = (near_x, again_x, other_x, swap(after(again_x, *ties)))
    near_0 = stack_rows(after(d[0], *ties), on_0, back_0)
    other_0 = swap(near_0)
    pre = forward(x_rows, w_gate, w_up, 0, pre)
    hidden_turned = hidden_of(pre).T

    ties = (again_0, on_1, back_1, other_0, hidden_turned)
    again_1 = on(on_1, *ties)
    rows_0 = (near_0, again_0, other_0, swap(after(again_0, *ties)))
    near_1 = stack_rows(after(d[1], *ties), on_1, back_1)
    other_1 = swap(near_1)
    projected, grad_down = down_terms(rows_0, w_down, hidden_turned, d_at[0])

    ties = (again_1, other_1, projected)
    rows_1 = (near_1, again_1, other_1, swap(after(again_1, *ties)))
    grad_down, grad_pre_gate, grad_pre_up, row_gate = down_end(
        rows_1, w_down, hidden_turned, pre, d_at[1], projected, grad_down
    )
    returned = return_rows(row_gate).reshape(columns, CAP)
    grads = up_terms(x_rows, raw_rows, grad_pre_gate, grad_pre_up)

    slot_values = jnp.sum(jnp.where(slot_hot, returned[None], 0.0), axis=2)
    picked = jnp.sum(jnp.where(matches, slot_values[:, None, :], 0.0), axis=2)
    gate_grad = picked / gates
    return *grads, grad_down, gate_grad


def solution(mesh):
    mesh = Mesh(mesh.devices.reshape(NX, NC, NZ, NY), ("x", "core", "z", "y"))
    tokens = P(("x", "core", "z", "y"), None)
    wide = P(("z", "y"), None, ("x", "core"))
    deep = P(("z", "y"), ("x", "core"), None)
    return jax.shard_map(
        per_device,
        mesh=mesh,
        in_specs=(tokens, tokens, tokens, tokens, wide, wide, deep),
        out_specs=(wide, wide, deep, tokens),
        check_vma=False,
    )
```

```python
import math

import jax
import jax.numpy as jnp
from jax import lax
from jax.experimental import pallas as pl
from jax.experimental.pallas import tpu as pltpu
from jax.sharding import Mesh, PartitionSpec as P

GROUPS = 8
CAP = 8
GROUP_SIZE = 32
NX, NC, NZ, NY = 4, 2, 4, 4

X_RAW, X_REST = 1792, 5376
BLOCK, END_BLOCK = 1792, 896
PARAMS = pltpu.CompilerParams(vmem_limit_bytes=62 * 2**20)


def after(x, *others):
    return x if not others else lax.optimization_barrier((x, *others))[0]


def shift(x, axis, by):
    n = lax.axis_size(axis)
    return lax.ppermute(x, axis, [(i, (i + by) % n) for i in range(n)])


def exchange_yz(tiles):
    return lax.all_to_all(tiles, ("z", "y"), 0, 0, tiled=True).reshape(-1, tiles.shape[2])


def hop(x, by):
    pairs = [(i * NC + c, (i + by * (1 - 2 * c)) % NX * NC + c) for i in range(NX) for c in range(NC)]
    return lax.ppermute(x, ("x", "core"), pairs)


SMALL = pl.CostEstimate(flops=1, bytes_accessed=1, transcendentals=0)
ANY = pl.BlockSpec(memory_space=pl.ANY)


def whole_parts(parts):
    return [part if isinstance(part, tuple) else (part, 0, part.shape[1]) for part in parts]


def row_specs(parts, block, step=lambda i: i):
    return [
        pl.BlockSpec((part.shape[0], block), lambda i, first=at // block: (0, first + step(i))) for part, at, _ in parts
    ]


def joined(refs):
    return jnp.concatenate([ref[...] for ref in refs])


def forward(parts, w_gate, w_up, at, all_rows, row=0, pre=None):
    parts = whole_parts(parts)
    size, count = parts[0][2], len(parts)
    rows = sum(part.shape[0] for part, _, _ in parts)
    width = w_gate.shape[2]
    block = math.gcd(BLOCK, size, at)
    first = at // block

    def kernel(*refs):
        out_ref = refs[-1]

        @pl.when(pl.program_id(0) == 0)
        def _():
            out_ref[...] = jnp.zeros_like(out_ref)

        x = joined(refs[2 : 2 + count])
        for j, w_ref in enumerate(refs[:2]):
            out_ref[:, j * width : (j + 1) * width] += jnp.dot(x, w_ref[0], preferred_element_type=jnp.float32)

    return pl.pallas_call(
        kernel,
        grid=(size // block,),
        in_specs=[pl.BlockSpec((1, block, width), lambda i: (0, first + i, 0))] * 2
        + row_specs(parts, block)
        + ([] if pre is None else [ANY]),
        out_specs=pl.BlockSpec((rows, 2 * width), lambda i: (row // rows, 0)),
        out_shape=jax.ShapeDtypeStruct((all_rows, 2 * width), jnp.float32),
        input_output_aliases={} if pre is None else {2 + count: 0},
        compiler_params=PARAMS,
        cost_estimate=SMALL,
    )(w_gate, w_up, *[part[0] for part in parts], *(() if pre is None else (pre,)))


def forward_end(parts, w_gate, w_up, at, pre):
    parts = whole_parts(parts)
    size, count = parts[0][2], len(parts)
    rows = pre.shape[0]
    width = w_gate.shape[2]
    block = math.gcd(END_BLOCK, size, at)
    first, steps = at // block, size // block
    strip = 128

    def kernel(*refs):
        pre_ref = refs[2 + count]
        activated_ref, slope_ref, hidden_ref, turned_ref, total = refs[-5:]

        @pl.when(pl.program_id(0) == 0)
        def _():
            total[...] = pre_ref[...]

        x = joined(refs[2 : 2 + count])
        for j, w_ref in enumerate(refs[:2]):
            total[:, j * width : (j + 1) * width] += jnp.dot(x, w_ref[0], preferred_element_type=jnp.float32)

        @pl.when(pl.program_id(0) == steps - 1)
        def _():
            for k in range(0, rows, strip):
                place = slice(k, k + strip)
                pre_gate, pre_up = total[place, :width], total[place, width:]
                sig = jax.nn.sigmoid(pre_gate)
                activated = pre_gate * sig
                hidden = (activated * pre_up).astype(jnp.bfloat16)
                activated_ref[place] = activated
                slope_ref[place] = pre_up * sig * (1.0 + pre_gate * (1.0 - sig))
                hidden_ref[place] = hidden
                turned_ref[:, place] = hidden.T

    def whole(*shape):
        return pl.BlockSpec(shape, lambda i: (0, 0))

    flat = jax.ShapeDtypeStruct((rows, width), jnp.float32)
    return pl.pallas_call(
        kernel,
        grid=(steps,),
        in_specs=[pl.BlockSpec((1, block, width), lambda i: (0, first + i, 0))] * 2
        + row_specs(parts, block)
        + [whole(*pre.shape)],
        out_specs=[whole(rows, width)] * 3 + [whole(width, rows)],
        out_shape=[
            flat,
            flat,
            jax.ShapeDtypeStruct((rows, width), jnp.bfloat16),
            jax.ShapeDtypeStruct((width, rows), jnp.bfloat16),
        ],
        scratch_shapes=[pltpu.VMEM(pre.shape, jnp.float32)],
        compiler_params=PARAMS,
        cost_estimate=SMALL,
    )(w_gate, w_up, *[part[0] for part in parts], pre)


def down_terms(parts, w_down, turned, activated, slope, hidden, order):
    parts = whole_parts(parts)
    size, count = parts[0][2], len(parts)
    rows, width = hidden.shape
    block = math.gcd(BLOCK, size)
    steps = size // block
    strip = rows // (NX * NC)

    def kernel(*refs):
        order_ref, down_ref, turned_ref = refs[:3]
        late_refs = refs[3:6]
        grad_ref, gate_ref, up_ref, row_ref, projected_ref = refs[-9:-4]
        held, sems = refs[-4:-1], refs[-1]
        copies = [pltpu.make_async_copy(late, own, sems.at[k]) for k, (late, own) in enumerate(zip(late_refs, held))]

        @pl.when(pl.program_id(0) == 0)
        def _():
            for copy in copies:
                copy.start()
            projected_ref[...] = jnp.zeros_like(projected_ref)

        dy = joined(refs[6 : 6 + count])
        projected_ref[...] += lax.dot_general(
            dy, down_ref[0], (((1,), (1,)), ((), ())), preferred_element_type=jnp.float32
        )
        grad_ref[0] = jnp.dot(turned_ref[...], dy, preferred_element_type=jnp.float32).astype(jnp.bfloat16)

        @pl.when(pl.program_id(0) == steps - 1)
        def _():
            for copy in copies:
                copy.wait()
            activated_ref, slope_ref, hidden_ref = held

            def some(k, _):
                at_rows = pl.ds(pl.multiple_of(k * strip, strip), strip)
                projected = projected_ref[at_rows]
                gate_ref[at_rows] = (projected * slope_ref[at_rows]).astype(jnp.bfloat16)
                up_ref[at_rows] = (projected * activated_ref[at_rows]).astype(jnp.bfloat16)
                sums = jnp.sum(hidden_ref[at_rows].astype(jnp.float32) * projected, axis=1, keepdims=True)
                row_ref[pl.ds(order_ref[k], 1)] = jnp.broadcast_to(sums, (strip, strip)).T[:1]
                return 0

            lax.fori_loop(0, rows // strip, some, 0)

    def whole(*shape):
        return pl.BlockSpec(shape, lambda i: (0, 0))

    wide = pl.BlockSpec((1, width, block), lambda i: (0, 0, i))
    grad = jax.ShapeDtypeStruct((rows, width), jnp.bfloat16)
    late = (activated, slope, hidden)
    return pl.pallas_call(
        kernel,
        grid=(steps,),
        in_specs=[pl.BlockSpec(memory_space=pltpu.SMEM), wide, whole(width, rows)]
        + [ANY] * len(late)
        + row_specs(parts, block),
        out_specs=[wide, whole(rows, width), whole(rows, width), whole(NX * NC, strip)],
        out_shape=[
            jax.ShapeDtypeStruct(w_down.shape, jnp.bfloat16),
            grad,
            grad,
            jax.ShapeDtypeStruct((NX * NC, strip), jnp.float32),
        ],
        scratch_shapes=[pltpu.VMEM((rows, width), jnp.float32)]
        + [pltpu.VMEM(a.shape, a.dtype) for a in late]
        + [pltpu.SemaphoreType.DMA((len(late),))],
        compiler_params=PARAMS,
        cost_estimate=SMALL,
    )(order, w_down, turned, *late, *[part[0] for part in parts])


def up_terms(parts, last_parts, grad_pre_gate, grad_pre_up):
    rows, width = grad_pre_gate.shape
    parts, last_parts = whole_parts(parts), whole_parts(last_parts)
    count, size, last = len(parts), parts[0][2], last_parts[0][2]
    block = math.gcd(BLOCK, size, last)
    steps, last_steps = size // block, last // block

    def kernel(*refs):
        out_refs = refs[-2:]

        def write(row_refs):
            x = joined(row_refs)
            for pre_ref, out_ref in zip(refs[:2], out_refs):
                out_ref[0] = lax.dot_general(
                    x, pre_ref[...], (((0,), (0,)), ((), ())), preferred_element_type=jnp.float32
                ).astype(jnp.bfloat16)

        pl.when(pl.program_id(0) < steps)(lambda: write(refs[2 : 2 + count]))
        pl.when(pl.program_id(0) >= steps)(lambda: write(refs[2 + count : -2]))

    out = jax.ShapeDtypeStruct((1, size + last, width), jnp.bfloat16)
    whole = pl.BlockSpec((rows, width), lambda i: (0, 0))
    return pl.pallas_call(
        kernel,
        grid=(steps + last_steps,),
        in_specs=[whole, whole]
        + row_specs(parts, block, lambda i: jnp.minimum(i, steps - 1))
        + row_specs(last_parts, block, lambda i: jnp.maximum(i - steps, 0)),
        out_specs=[pl.BlockSpec((1, block, width), lambda i: (0, i, 0))] * 2,
        out_shape=[out, out],
        compiler_params=PARAMS,
        cost_estimate=SMALL,
    )(grad_pre_gate, grad_pre_up, *[part[0] for part in (*parts, *last_parts)])


def row_order():
    x, core = lax.axis_index("x"), lax.axis_index("core")
    near = [(c, by) for c in (core, 1 - core) for by in (0, 1, -1)]
    return jnp.stack([(x - by * (1 - 2 * c)) % NX * NC + c for c, by in near + [(core, 2), (1 - core, 2)]]).astype(jnp.int32)


def return_rows(row_gate):
    got = lax.all_to_all(row_gate.reshape(-1, CAP), ("x", "core", "z", "y"), 0, 0, tiled=True)
    return jnp.sum(got.reshape(NC * NX, NZ * NY, CAP), axis=0)


def per_device(tokens, cotangent, expert_ids, gate_probs, w_gate, w_up, w_down):
    tok_here = tokens.shape[0]
    columns = NZ * NY
    experts = jnp.arange(columns, dtype=jnp.int32)
    routed = experts % GROUPS * GROUP_SIZE + experts // GROUPS
    matches = expert_ids[:, :, None] == routed[None, None, :]
    routed_here = jnp.any(matches, axis=1).astype(jnp.int32)
    slot_rank = jnp.cumsum(routed_here, axis=0) - routed_here
    slot_hot = jnp.logical_and(
        slot_rank[:, :, None] == jnp.arange(CAP, dtype=jnp.int32)[None, None, :],
        routed_here[:, :, None] == 1,
    )
    gates = gate_probs.astype(jnp.float32)
    gate_sel = jnp.sum(jnp.where(matches, gates[:, :, None], 0.0), axis=1)
    placer = slot_hot.astype(jnp.bfloat16).reshape(tok_here, columns * CAP)
    placer_gate = (
        jnp.where(slot_hot, gate_sel[:, :, None], 0.0).astype(jnp.bfloat16).reshape(tok_here, columns * CAP)
    )
    width = w_gate.shape[2]

    def tiles_of(place, source, at, size):
        tiles = lax.dot_general(
            place, source[:, at : at + size], (((0,), (0,)), ((), ())), preferred_element_type=jnp.float32
        )
        return tiles.astype(jnp.bfloat16).reshape(columns, CAP, size)

    def on(block, *ties):
        return hop(after(block, *ties), 1)

    def back(block, *ties):
        return hop(after(block, *ties), -1)

    def swap(part):
        return shift(part, "core", 1)

    features = tokens.shape[1]
    all_rows = NX * NC * columns * CAP
    split = all_rows * 3 // 4

    raw = tiles_of(placer, tokens, X_REST, X_RAW).reshape(-1, X_RAW)
    on_r, back_r = hop(raw, 1), hop(raw, -1)
    x = exchange_yz(after(tiles_of(placer, tokens, 0, X_REST), raw))
    rounds = [part.reshape(columns, CAP, X_RAW) for part in (raw, on_r, back_r, hop(on_r, 1))]
    dy = tiles_of(placer_gate, cotangent, 0, features)
    rounds = jnp.concatenate(rounds, axis=2)

    ties = (x, rounds, dy, row_order())
    order = lax.optimization_barrier(ties)[3]
    on_x, back_x = on(x, *ties), back(x, *ties)
    other_x = swap(after(x, *ties))
    dy = exchange_yz(after(dy, *ties))

    ties = (dy, on_x, back_x, other_x)
    again_x, on_dy, back_dy = on(on_x, *ties), on(dy, *ties), back(dy, *ties)
    rounds = exchange_yz(after(rounds, *ties))
    near_x = lax.optimization_barrier((x, on_x, back_x, *ties))[:3]
    near_x = (*near_x, other_x, swap(near_x[1]), swap(near_x[2]))
    other_dy = swap(after(dy, *ties))
    pre = forward(near_x, w_gate, w_up, 0, all_rows)

    ties = (rounds, again_x, on_dy, back_dy, other_dy, pre)
    again_dy = on(on_dy, *ties)
    again_x = (after(again_x, *ties), swap(after(again_x, *ties)))
    rounds = after(rounds, *ties)
    rounds = (rounds, swap(rounds))
    raw_rows = [(part, k * X_RAW, X_RAW) for ks in ((0, 1, 2), (3,)) for part in rounds for k in ks]
    near_dy = lax.optimization_barrier((dy, on_dy, back_dy, *ties))[:3]
    near_dy = (*near_dy, other_dy, swap(near_dy[1]), swap(near_dy[2]))
    pre = forward(again_x, w_gate, w_up, 0, all_rows, split, pre)
    activated, slope, hidden, turned = forward_end(raw_rows, w_gate, w_up, X_REST, pre)

    ties = (again_dy, *near_dy, turned)
    again_dy = (again_dy, swap(after(again_dy, *ties)))
    grad_down, grad_pre_gate, grad_pre_up, row_gate = down_terms(
        (*near_dy, *again_dy), w_down, turned, activated, slope, hidden, order
    )
    returned = return_rows(row_gate).reshape(columns, CAP)
    grads = up_terms((*near_x, *again_x), raw_rows, grad_pre_gate, grad_pre_up)

    slot_values = jnp.sum(jnp.where(slot_hot, returned[None], 0.0), axis=2)
    picked = jnp.sum(jnp.where(matches, slot_values[:, None, :], 0.0), axis=2)
    gate_grad = picked / gates
    return *grads, grad_down, gate_grad


def solution(mesh):
    mesh = Mesh(mesh.devices.reshape(NX, NC, NZ, NY), ("x", "core", "z", "y"))
    tokens = P(("x", "core", "z", "y"), None)
    wide = P(("z", "y"), None, ("x", "core"))
    deep = P(("z", "y"), ("x", "core"), None)
    return jax.shard_map(
        per_device,
        mesh=mesh,
        in_specs=(tokens, tokens, tokens, tokens, wide, wide, deep),
        out_specs=(wide, wide, deep, tokens),
        check_vma=False,
    )
```

```python
import math

import jax
import jax.numpy as jnp
from jax import lax
from jax.experimental import pallas as pl
from jax.experimental.pallas import tpu as pltpu
from jax.sharding import Mesh, PartitionSpec as P

GROUPS = 8
CAP = 8
GROUP_SIZE = 32
NX, NC, NZ, NY = 4, 2, 4, 4

X_RAW, X_REST = 1792, 5376
BLOCK, END_BLOCK = 1792, 896
PARAMS = pltpu.CompilerParams(vmem_limit_bytes=63 * 2**20)


def after(x, *others):
    return x if not others else lax.optimization_barrier((x, *others))[0]


def shift(x, axis, by):
    n = lax.axis_size(axis)
    return lax.ppermute(x, axis, [(i, (i + by) % n) for i in range(n)])


def exchange_yz(tiles):
    return lax.all_to_all(tiles, ("z", "y"), 0, 0, tiled=True).reshape(-1, tiles.shape[2])


def hop(x, by):
    pairs = [(i * NC + c, (i + by * (1 - 2 * c)) % NX * NC + c) for i in range(NX) for c in range(NC)]
    return lax.ppermute(x, ("x", "core"), pairs)


SMALL = pl.CostEstimate(flops=1, bytes_accessed=1, transcendentals=0)
ANY = pl.BlockSpec(memory_space=pl.ANY)


def whole_parts(parts):
    return [part if isinstance(part, tuple) else (part, 0, part.shape[1]) for part in parts]


def row_specs(parts, block, step=lambda i: i):
    return [
        pl.BlockSpec((part.shape[0], block), lambda i, first=at // block: (0, first + step(i))) for part, at, _ in parts
    ]


def joined(refs):
    return jnp.concatenate([ref[...] for ref in refs])


def forward(parts, w_gate, w_up, at, all_rows, row=0, pre=None):
    parts = whole_parts(parts)
    size, count = parts[0][2], len(parts)
    rows = sum(part.shape[0] for part, _, _ in parts)
    width = w_gate.shape[2]
    block = math.gcd(BLOCK, size, at)
    first = at // block

    def kernel(*refs):
        out_ref = refs[-1]

        @pl.when(pl.program_id(0) == 0)
        def _():
            out_ref[...] = jnp.zeros_like(out_ref)

        x = joined(refs[2 : 2 + count])
        for j, w_ref in enumerate(refs[:2]):
            out_ref[:, j * width : (j + 1) * width] += jnp.dot(x, w_ref[0], preferred_element_type=jnp.float32)

    return pl.pallas_call(
        kernel,
        grid=(size // block,),
        in_specs=[pl.BlockSpec((1, block, width), lambda i: (0, first + i, 0))] * 2
        + row_specs(parts, block)
        + ([] if pre is None else [ANY]),
        out_specs=pl.BlockSpec((rows, 2 * width), lambda i: (row // rows, 0)),
        out_shape=jax.ShapeDtypeStruct((all_rows, 2 * width), jnp.float32),
        input_output_aliases={} if pre is None else {2 + count: 0},
        compiler_params=PARAMS,
        cost_estimate=SMALL,
    )(w_gate, w_up, *[part[0] for part in parts], *(() if pre is None else (pre,)))


def forward_end(parts, w_gate, w_up, at, pre):
    parts = whole_parts(parts)
    size, count = parts[0][2], len(parts)
    rows = pre.shape[0]
    width = w_gate.shape[2]
    block = math.gcd(END_BLOCK, size, at)
    first, steps = at // block, size // block
    strip = 128

    def kernel(*refs):
        pre_ref = refs[2 + count]
        activated_ref, slope_ref, hidden_ref, turned_ref, total = refs[-5:]

        @pl.when(pl.program_id(0) == 0)
        def _():
            total[...] = pre_ref[...]

        x = joined(refs[2 : 2 + count])
        for j, w_ref in enumerate(refs[:2]):
            total[:, j * width : (j + 1) * width] += jnp.dot(x, w_ref[0], preferred_element_type=jnp.float32)

        @pl.when(pl.program_id(0) == steps - 1)
        def _():
            for k in range(0, rows, strip):
                place = slice(k, k + strip)
                pre_gate, pre_up = total[place, :width], total[place, width:]
                sig = jax.nn.sigmoid(pre_gate)
                activated = pre_gate * sig
                hidden = (activated * pre_up).astype(jnp.bfloat16)
                activated_ref[place] = activated
                slope_ref[place] = pre_up * sig * (1.0 + pre_gate * (1.0 - sig))
                hidden_ref[place] = hidden
                turned_ref[:, place] = hidden.T

    def whole(*shape):
        return pl.BlockSpec(shape, lambda i: (0, 0))

    flat = jax.ShapeDtypeStruct((rows, width), jnp.float32)
    return pl.pallas_call(
        kernel,
        grid=(steps,),
        in_specs=[pl.BlockSpec((1, block, width), lambda i: (0, first + i, 0))] * 2
        + row_specs(parts, block)
        + [whole(*pre.shape)],
        out_specs=[whole(rows, width)] * 3 + [whole(width, rows)],
        out_shape=[
            flat,
            flat,
            jax.ShapeDtypeStruct((rows, width), jnp.bfloat16),
            jax.ShapeDtypeStruct((width, rows), jnp.bfloat16),
        ],
        scratch_shapes=[pltpu.VMEM(pre.shape, jnp.float32)],
        compiler_params=PARAMS,
        cost_estimate=SMALL,
    )(w_gate, w_up, *[part[0] for part in parts], pre)


def project(parts, w_down):
    parts = whole_parts(parts)
    size = parts[0][2]
    rows, width = sum(part.shape[0] for part, _, _ in parts), w_down.shape[1]
    block = math.gcd(BLOCK, size)

    def kernel(down_ref, *refs):
        out_ref = refs[-1]

        @pl.when(pl.program_id(0) == 0)
        def _():
            out_ref[...] = jnp.zeros_like(out_ref)

        out_ref[...] += lax.dot_general(
            joined(refs[:-1]), down_ref[0], (((1,), (1,)), ((), ())), preferred_element_type=jnp.float32
        )

    return pl.pallas_call(
        kernel,
        grid=(size // block,),
        in_specs=[pl.BlockSpec((1, width, block), lambda i: (0, 0, i))] + row_specs(parts, block),
        out_specs=pl.BlockSpec((rows, width), lambda i: (0, 0)),
        out_shape=jax.ShapeDtypeStruct((rows, width), jnp.float32),
        compiler_params=PARAMS,
        cost_estimate=SMALL,
    )(w_down, *[part[0] for part in parts])


def down_terms(parts, w_down, turned, projected, activated, slope, hidden, order):
    parts = whole_parts(parts)
    size, count = parts[0][2], len(parts)
    rows, width = hidden.shape
    block = math.gcd(BLOCK, size)
    steps = size // block
    strip, known = rows // (NX * NC), projected.shape[0]
    late = (activated, slope, hidden, projected)
    n_late = len(late)

    def kernel(*refs):
        order_ref, down_ref, turned_ref = refs[:3]
        late_refs = refs[3 : 3 + n_late]
        grad_ref, gate_ref, up_ref, row_ref, projected_ref = refs[-6 - n_late : -1 - n_late]
        held, sems = refs[-1 - n_late : -1], refs[-1]
        copies = [pltpu.make_async_copy(late, own, sems.at[k]) for k, (late, own) in enumerate(zip(late_refs, held))]

        @pl.when(pl.program_id(0) == 0)
        def _():
            for copy in copies:
                copy.start()
            projected_ref[known:] = jnp.zeros_like(projected_ref[known:])

        dy = joined(refs[3 + n_late : 3 + n_late + count])
        projected_ref[known:] += lax.dot_general(
            dy[known:], down_ref[0], (((1,), (1,)), ((), ())), preferred_element_type=jnp.float32
        )
        grad_ref[0] = jnp.dot(turned_ref[...], dy, preferred_element_type=jnp.float32).astype(jnp.bfloat16)

        @pl.when(pl.program_id(0) == steps - 1)
        def _():
            for copy in copies:
                copy.wait()
            activated_ref, slope_ref, hidden_ref, known_ref = held
            projected_ref[:known] = known_ref[...]
            row = lax.broadcasted_iota(jnp.int32, (strip // CAP, strip), 1)
            source = lax.broadcasted_iota(jnp.int32, (strip // CAP, strip), 0)
            of_source = (row // CAP == source).astype(jnp.float32)
            row = lax.broadcasted_iota(jnp.int32, (strip, CAP), 0)
            slot = lax.broadcasted_iota(jnp.int32, (strip, CAP), 1)
            in_slot = row % CAP == slot

            for k in range(rows // strip):
                at_rows = slice(k * strip, (k + 1) * strip)
                projected = projected_ref[at_rows]
                gate_ref[at_rows] = (projected * slope_ref[at_rows]).astype(jnp.bfloat16)
                up_ref[at_rows] = (projected * activated_ref[at_rows]).astype(jnp.bfloat16)
                sums = jnp.sum(hidden_ref[at_rows].astype(jnp.float32) * projected, axis=1, keepdims=True)
                place = pl.ds(pl.multiple_of(order_ref[k] * (strip // CAP), strip // CAP), strip // CAP)
                row_ref[place] = jnp.dot(
                    of_source, jnp.where(in_slot, sums, 0.0), precision=lax.Precision.HIGHEST
                )

    def whole(*shape):
        return pl.BlockSpec(shape, lambda i: (0, 0))

    wide = pl.BlockSpec((1, width, block), lambda i: (0, 0, i))
    grad = jax.ShapeDtypeStruct((rows, width), jnp.bfloat16)
    return pl.pallas_call(
        kernel,
        grid=(steps,),
        in_specs=[pl.BlockSpec(memory_space=pltpu.SMEM), wide, whole(width, rows)]
        + [ANY] * len(late)
        + row_specs(parts, block),
        out_specs=[wide, whole(rows, width), whole(rows, width), whole(rows // CAP, CAP)],
        out_shape=[
            jax.ShapeDtypeStruct(w_down.shape, jnp.bfloat16),
            grad,
            grad,
            jax.ShapeDtypeStruct((rows // CAP, CAP), jnp.float32),
        ],
        scratch_shapes=[pltpu.VMEM((rows, width), jnp.float32)]
        + [pltpu.VMEM(a.shape, a.dtype) for a in late]
        + [pltpu.SemaphoreType.DMA((len(late),))],
        compiler_params=PARAMS,
        cost_estimate=SMALL,
    )(order, w_down, turned, *late, *[part[0] for part in parts])


def up_terms(parts, last_parts, grad_pre_gate, grad_pre_up):
    rows, width = grad_pre_gate.shape
    parts, last_parts = whole_parts(parts), whole_parts(last_parts)
    count, size, last = len(parts), parts[0][2], last_parts[0][2]
    block = math.gcd(BLOCK, size, last)
    steps, last_steps = size // block, last // block

    def kernel(*refs):
        out_refs = refs[-2:]

        def write(row_refs):
            x = joined(row_refs)
            for pre_ref, out_ref in zip(refs[:2], out_refs):
                out_ref[0] = lax.dot_general(
                    x, pre_ref[...], (((0,), (0,)), ((), ())), preferred_element_type=jnp.float32
                ).astype(jnp.bfloat16)

        pl.when(pl.program_id(0) < steps)(lambda: write(refs[2 : 2 + count]))
        pl.when(pl.program_id(0) >= steps)(lambda: write(refs[2 + count : -2]))

    out = jax.ShapeDtypeStruct((1, size + last, width), jnp.bfloat16)
    whole = pl.BlockSpec((rows, width), lambda i: (0, 0))
    return pl.pallas_call(
        kernel,
        grid=(steps + last_steps,),
        in_specs=[whole, whole]
        + row_specs(parts, block, lambda i: jnp.minimum(i, steps - 1))
        + row_specs(last_parts, block, lambda i: jnp.maximum(i - steps, 0)),
        out_specs=[pl.BlockSpec((1, block, width), lambda i: (0, i, 0))] * 2,
        out_shape=[out, out],
        compiler_params=PARAMS,
        cost_estimate=SMALL,
    )(grad_pre_gate, grad_pre_up, *[part[0] for part in (*parts, *last_parts)])


def row_order():
    x, core = lax.axis_index("x"), lax.axis_index("core")
    near = [(c, by) for c in (core, 1 - core) for by in (0, 1, -1)]
    return jnp.stack([(x - by * (1 - 2 * c)) % NX * NC + c for c, by in near + [(core, 2), (1 - core, 2)]]).astype(jnp.int32)


def return_rows(row_gate):
    got = lax.all_to_all(row_gate, ("x", "core", "z", "y"), 0, 0, tiled=True)
    return jnp.sum(got.reshape(NC * NX, NZ * NY, CAP), axis=0)


def per_device(tokens, cotangent, expert_ids, gate_probs, w_gate, w_up, w_down):
    tok_here = tokens.shape[0]
    columns = NZ * NY
    experts = jnp.arange(columns, dtype=jnp.int32)
    routed = experts % GROUPS * GROUP_SIZE + experts // GROUPS
    matches = expert_ids[:, :, None] == routed[None, None, :]
    routed_here = jnp.any(matches, axis=1).astype(jnp.int32)
    slot_rank = jnp.cumsum(routed_here, axis=0) - routed_here
    slot_hot = jnp.logical_and(
        slot_rank[:, :, None] == jnp.arange(CAP, dtype=jnp.int32)[None, None, :],
        routed_here[:, :, None] == 1,
    )
    gates = gate_probs.astype(jnp.float32)
    gate_sel = jnp.sum(jnp.where(matches, gates[:, :, None], 0.0), axis=1)
    placer = slot_hot.astype(jnp.bfloat16).reshape(tok_here, columns * CAP)
    placer_gate = (
        jnp.where(slot_hot, gate_sel[:, :, None], 0.0).astype(jnp.bfloat16).reshape(tok_here, columns * CAP)
    )
    width = w_gate.shape[2]

    def tiles_of(place, source, at, size):
        tiles = lax.dot_general(
            place, source[:, at : at + size], (((0,), (0,)), ((), ())), preferred_element_type=jnp.float32
        )
        return tiles.astype(jnp.bfloat16).reshape(columns, CAP, size)

    def on(block, *ties):
        return hop(after(block, *ties), 1)

    def back(block, *ties):
        return hop(after(block, *ties), -1)

    def swap(part):
        return shift(part, "core", 1)

    features = tokens.shape[1]
    all_rows = NX * NC * columns * CAP
    split = all_rows * 3 // 4

    raw = tiles_of(placer, tokens, X_REST, X_RAW).reshape(-1, X_RAW)
    on_r, back_r = hop(raw, 1), hop(raw, -1)
    x = exchange_yz(after(tiles_of(placer, tokens, 0, X_REST), raw))
    middle = raw.shape[0] // 2
    again_r = jnp.concatenate([hop(on_r[:middle], 1), hop(back_r[middle:], -1)])
    rounds = [part.reshape(columns, CAP, X_RAW) for part in (raw, on_r, back_r, again_r)]
    dy = tiles_of(placer_gate, cotangent, 0, features)
    rounds = jnp.concatenate(rounds, axis=2)

    ties = (x, rounds, dy, row_order())
    order = lax.optimization_barrier(ties)[3]
    on_x, back_x = on(x, *ties), back(x, *ties)
    other_x = swap(after(x, *ties))
    dy = exchange_yz(after(dy, *ties))

    ties = (dy, on_x, back_x, other_x)
    again_x, on_dy, back_dy = on(on_x, *ties), on(dy, *ties), back(dy, *ties)
    rounds = exchange_yz(after(rounds, *ties))
    near_x = lax.optimization_barrier((x, on_x, back_x, *ties))[:3]
    near_x = (*near_x, other_x, swap(near_x[1]), swap(near_x[2]))
    other_dy = swap(after(dy, *ties))
    pre = forward(near_x, w_gate, w_up, 0, all_rows)

    ties = (rounds, again_x, on_dy, back_dy, other_dy, pre)
    again_dy = on(on_dy, *ties)
    again_x = (after(again_x, *ties), swap(after(again_x, *ties)))
    rounds = after(rounds, *ties)
    rounds = (rounds, swap(rounds))
    raw_rows = [(part, k * X_RAW, X_RAW) for ks in ((0, 1, 2), (3,)) for part in rounds for k in ks]
    near_dy = lax.optimization_barrier((dy, on_dy, back_dy, *ties))[:3]
    near_dy = (*near_dy, other_dy, swap(near_dy[1]), swap(near_dy[2]))
    pre = forward(again_x, w_gate, w_up, 0, all_rows, split, pre)
    activated, slope, hidden, turned = forward_end(raw_rows, w_gate, w_up, X_REST, pre)

    known = project(near_dy[:4], w_down)

    ties = (again_dy, *near_dy, turned, known)
    again_dy = (again_dy, swap(after(again_dy, *ties)))
    grad_down, grad_pre_gate, grad_pre_up, row_gate = down_terms(
        (*near_dy, *again_dy), w_down, turned, known, activated, slope, hidden, order
    )
    returned = return_rows(row_gate).reshape(columns, CAP)
    grads = up_terms((*near_x, *again_x), raw_rows, grad_pre_gate, grad_pre_up)

    slot_values = jnp.sum(jnp.where(slot_hot, returned[None], 0.0), axis=2)
    picked = jnp.sum(jnp.where(matches, slot_values[:, None, :], 0.0), axis=2)
    gate_grad = picked / gates
    return *grads, grad_down, gate_grad


def solution(mesh):
    mesh = Mesh(mesh.devices.reshape(NX, NC, NZ, NY), ("x", "core", "z", "y"))
    tokens = P(("x", "core", "z", "y"), None)
    wide = P(("z", "y"), None, ("x", "core"))
    deep = P(("z", "y"), ("x", "core"), None)
    return jax.shard_map(
        per_device,
        mesh=mesh,
        in_specs=(tokens, tokens, tokens, tokens, wide, wide, deep),
        out_specs=(wide, wide, deep, tokens),
        check_vma=False,
    )
```

```python
import math

import jax
import jax.numpy as jnp
from jax import lax
from jax.experimental import pallas as pl
from jax.experimental.pallas import tpu as pltpu
from jax.sharding import Mesh, PartitionSpec as P

GROUPS = 8
CAP = 8
GROUP_SIZE = 32
NX, NC, NZ, NY = 4, 2, 4, 4

X_RAW, X_REST = 1792, 5376
BLOCK, END_BLOCK = 1792, 896
PARAMS = pltpu.CompilerParams(vmem_limit_bytes=63 * 2**20)


def after(x, *others):
    return x if not others else lax.optimization_barrier((x, *others))[0]


def shift(x, axis, by):
    n = lax.axis_size(axis)
    return lax.ppermute(x, axis, [(i, (i + by) % n) for i in range(n)])


def exchange_yz(tiles):
    return lax.all_to_all(tiles, ("z", "y"), 0, 0, tiled=True).reshape(-1, tiles.shape[2])


def hop(x, by):
    pairs = [(i * NC + c, (i + by * (1 - 2 * c)) % NX * NC + c) for i in range(NX) for c in range(NC)]
    return lax.ppermute(x, ("x", "core"), pairs)


SMALL = pl.CostEstimate(flops=1, bytes_accessed=1, transcendentals=0)
ANY = pl.BlockSpec(memory_space=pl.ANY)


def whole_parts(parts):
    return [part if isinstance(part, tuple) else (part, 0, part.shape[1]) for part in parts]


def row_specs(parts, block, step=lambda i: i):
    return [
        pl.BlockSpec((part.shape[0], block), lambda i, first=at // block: (0, first + step(i))) for part, at, _ in parts
    ]


def joined(refs):
    return jnp.concatenate([ref[...] for ref in refs])


def forward(parts, w_gate, w_up, at, all_rows, row=0, pre=None):
    parts = whole_parts(parts)
    size, count = parts[0][2], len(parts)
    rows = sum(part.shape[0] for part, _, _ in parts)
    width = w_gate.shape[2]
    block = math.gcd(BLOCK, size, at)
    first = at // block

    def kernel(*refs):
        out_ref = refs[-1]

        @pl.when(pl.program_id(0) == 0)
        def _():
            out_ref[...] = jnp.zeros_like(out_ref)

        x = joined(refs[2 : 2 + count])
        for j, w_ref in enumerate(refs[:2]):
            out_ref[:, j * width : (j + 1) * width] += jnp.dot(x, w_ref[0], preferred_element_type=jnp.float32)

    return pl.pallas_call(
        kernel,
        grid=(size // block,),
        in_specs=[pl.BlockSpec((1, block, width), lambda i: (0, first + i, 0))] * 2
        + row_specs(parts, block)
        + ([] if pre is None else [ANY]),
        out_specs=pl.BlockSpec((rows, 2 * width), lambda i: (row // rows, 0)),
        out_shape=jax.ShapeDtypeStruct((all_rows, 2 * width), jnp.float32),
        input_output_aliases={} if pre is None else {2 + count: 0},
        compiler_params=PARAMS,
        cost_estimate=SMALL,
    )(w_gate, w_up, *[part[0] for part in parts], *(() if pre is None else (pre,)))


def forward_end(parts, w_gate, w_up, at, pre):
    parts = whole_parts(parts)
    size, count = parts[0][2], len(parts)
    rows = pre.shape[0]
    width = w_gate.shape[2]
    block = math.gcd(END_BLOCK, size, at)
    first, steps = at // block, size // block
    strip = 128

    def kernel(*refs):
        pre_ref = refs[2 + count]
        activated_ref, slope_ref, hidden_ref, turned_ref, total = refs[-5:]

        @pl.when(pl.program_id(0) == 0)
        def _():
            total[...] = pre_ref[...]

        x = joined(refs[2 : 2 + count])
        for j, w_ref in enumerate(refs[:2]):
            total[:, j * width : (j + 1) * width] += jnp.dot(x, w_ref[0], preferred_element_type=jnp.float32)

        @pl.when(pl.program_id(0) == steps - 1)
        def _():
            for k in range(0, rows, strip):
                place = slice(k, k + strip)
                pre_gate, pre_up = total[place, :width], total[place, width:]
                sig = jax.nn.sigmoid(pre_gate)
                activated = pre_gate * sig
                hidden = (activated * pre_up).astype(jnp.bfloat16)
                activated_ref[place] = activated
                slope_ref[place] = pre_up * sig * (1.0 + pre_gate * (1.0 - sig))
                hidden_ref[place] = hidden
                turned_ref[:, place] = hidden.T

    def whole(*shape):
        return pl.BlockSpec(shape, lambda i: (0, 0))

    flat = jax.ShapeDtypeStruct((rows, width), jnp.float32)
    return pl.pallas_call(
        kernel,
        grid=(steps,),
        in_specs=[pl.BlockSpec((1, block, width), lambda i: (0, first + i, 0))] * 2
        + row_specs(parts, block)
        + [whole(*pre.shape)],
        out_specs=[whole(rows, width)] * 3 + [whole(width, rows)],
        out_shape=[
            flat,
            flat,
            jax.ShapeDtypeStruct((rows, width), jnp.bfloat16),
            jax.ShapeDtypeStruct((width, rows), jnp.bfloat16),
        ],
        scratch_shapes=[pltpu.VMEM(pre.shape, jnp.float32)],
        compiler_params=PARAMS,
        cost_estimate=SMALL,
    )(w_gate, w_up, *[part[0] for part in parts], pre)


def project(parts, w_down):
    parts = whole_parts(parts)
    size = parts[0][2]
    rows, width = sum(part.shape[0] for part, _, _ in parts), w_down.shape[1]
    block = math.gcd(BLOCK, size)

    def kernel(down_ref, *refs):
        out_ref = refs[-1]

        @pl.when(pl.program_id(0) == 0)
        def _():
            out_ref[...] = jnp.zeros_like(out_ref)

        out_ref[...] += lax.dot_general(
            joined(refs[:-1]), down_ref[0], (((1,), (1,)), ((), ())), preferred_element_type=jnp.float32
        )

    return pl.pallas_call(
        kernel,
        grid=(size // block,),
        in_specs=[pl.BlockSpec((1, width, block), lambda i: (0, 0, i))] + row_specs(parts, block),
        out_specs=pl.BlockSpec((rows, width), lambda i: (0, 0)),
        out_shape=jax.ShapeDtypeStruct((rows, width), jnp.float32),
        compiler_params=PARAMS,
        cost_estimate=SMALL,
    )(w_down, *[part[0] for part in parts])


def down_terms(parts, w_down, turned, projected, activated, slope, hidden, order):
    parts = whole_parts(parts)
    size, count = parts[0][2], len(parts)
    rows, width = hidden.shape
    block = math.gcd(BLOCK, size)
    steps = size // block
    strip, known = rows // (NX * NC), projected.shape[0]
    late = (activated, slope, hidden, projected)
    n_late = len(late)

    def kernel(*refs):
        order_ref, down_ref, turned_ref = refs[:3]
        late_refs = refs[3 : 3 + n_late]
        grad_ref, gate_ref, up_ref, row_ref, projected_ref = refs[-6 - n_late : -1 - n_late]
        held, sems = refs[-1 - n_late : -1], refs[-1]
        copies = [pltpu.make_async_copy(late, own, sems.at[k]) for k, (late, own) in enumerate(zip(late_refs, held))]

        @pl.when(pl.program_id(0) == 0)
        def _():
            for copy in copies:
                copy.start()
            projected_ref[known:] = jnp.zeros_like(projected_ref[known:])

        dy = joined(refs[3 + n_late : 3 + n_late + count])
        projected_ref[known:] += lax.dot_general(
            dy[known:], down_ref[0], (((1,), (1,)), ((), ())), preferred_element_type=jnp.float32
        )
        grad_ref[0] = jnp.dot(turned_ref[...], dy, preferred_element_type=jnp.float32).astype(jnp.bfloat16)

        @pl.when(pl.program_id(0) == steps - 1)
        def _():
            for copy in copies:
                copy.wait()
            activated_ref, slope_ref, hidden_ref, known_ref = held
            projected_ref[:known] = known_ref[...]
            row = lax.broadcasted_iota(jnp.int32, (strip // CAP, strip), 1)
            source = lax.broadcasted_iota(jnp.int32, (strip // CAP, strip), 0)
            of_source = (row // CAP == source).astype(jnp.float32)
            row = lax.broadcasted_iota(jnp.int32, (strip, CAP), 0)
            slot = lax.broadcasted_iota(jnp.int32, (strip, CAP), 1)
            in_slot = row % CAP == slot

            for k in range(rows // strip):
                at_rows = slice(k * strip, (k + 1) * strip)
                projected = projected_ref[at_rows]
                gate_ref[at_rows] = (projected * slope_ref[at_rows]).astype(jnp.bfloat16)
                up_ref[at_rows] = (projected * activated_ref[at_rows]).astype(jnp.bfloat16)
                sums = jnp.sum(hidden_ref[at_rows].astype(jnp.float32) * projected, axis=1, keepdims=True)
                place = pl.ds(pl.multiple_of(order_ref[k] * (strip // CAP), strip // CAP), strip // CAP)
                row_ref[place] = jnp.dot(
                    of_source, jnp.where(in_slot, sums, 0.0), precision=lax.Precision.HIGHEST
                )

    def whole(*shape):
        return pl.BlockSpec(shape, lambda i: (0, 0))

    wide = pl.BlockSpec((1, width, block), lambda i: (0, 0, i))
    grad = jax.ShapeDtypeStruct((rows, width), jnp.bfloat16)
    return pl.pallas_call(
        kernel,
        grid=(steps,),
        in_specs=[pl.BlockSpec(memory_space=pltpu.SMEM), wide, whole(width, rows)]
        + [ANY] * len(late)
        + row_specs(parts, block),
        out_specs=[wide, whole(rows, width), whole(rows, width), whole(rows // CAP, CAP)],
        out_shape=[
            jax.ShapeDtypeStruct(w_down.shape, jnp.bfloat16),
            grad,
            grad,
            jax.ShapeDtypeStruct((rows // CAP, CAP), jnp.float32),
        ],
        scratch_shapes=[pltpu.VMEM((rows, width), jnp.float32)]
        + [pltpu.VMEM(a.shape, a.dtype) for a in late]
        + [pltpu.SemaphoreType.DMA((len(late),))],
        compiler_params=PARAMS,
        cost_estimate=SMALL,
    )(order, w_down, turned, *late, *[part[0] for part in parts])


def up_terms(parts, last_parts, grad_pre_gate, grad_pre_up):
    rows, width = grad_pre_gate.shape
    parts, last_parts = whole_parts(parts), whole_parts(last_parts)
    count, size, last = len(parts), parts[0][2], last_parts[0][2]
    block = math.gcd(BLOCK, size, last)
    steps, last_steps = size // block, last // block

    def kernel(*refs):
        out_refs = refs[-2:]

        def write(row_refs):
            x = joined(row_refs)
            for pre_ref, out_ref in zip(refs[:2], out_refs):
                out_ref[0] = lax.dot_general(
                    x, pre_ref[...], (((0,), (0,)), ((), ())), preferred_element_type=jnp.float32
                ).astype(jnp.bfloat16)

        pl.when(pl.program_id(0) < steps)(lambda: write(refs[2 : 2 + count]))
        pl.when(pl.program_id(0) >= steps)(lambda: write(refs[2 + count : -2]))

    out = jax.ShapeDtypeStruct((1, size + last, width), jnp.bfloat16)
    whole = pl.BlockSpec((rows, width), lambda i: (0, 0))
    return pl.pallas_call(
        kernel,
        grid=(steps + last_steps,),
        in_specs=[whole, whole]
        + row_specs(parts, block, lambda i: jnp.minimum(i, steps - 1))
        + row_specs(last_parts, block, lambda i: jnp.maximum(i - steps, 0)),
        out_specs=[pl.BlockSpec((1, block, width), lambda i: (0, i, 0))] * 2,
        out_shape=[out, out],
        compiler_params=PARAMS,
        cost_estimate=SMALL,
    )(grad_pre_gate, grad_pre_up, *[part[0] for part in (*parts, *last_parts)])


def row_order():
    x, core = lax.axis_index("x"), lax.axis_index("core")
    near = [(c, by) for c in (core, 1 - core) for by in (0, 1, -1)]
    return jnp.stack([(x - by * (1 - 2 * c)) % NX * NC + c for c, by in near + [(core, 2), (1 - core, 2)]]).astype(jnp.int32)


def return_rows(row_gate):
    got = lax.all_to_all(row_gate, ("x", "core", "z", "y"), 0, 0, tiled=True)
    return jnp.sum(got.reshape(NC * NX, NZ * NY, CAP), axis=0)


def per_device(tokens, cotangent, expert_ids, gate_probs, w_gate, w_up, w_down):
    tok_here = tokens.shape[0]
    columns = NZ * NY
    experts = jnp.arange(columns, dtype=jnp.int32)
    routed = experts % GROUPS * GROUP_SIZE + experts // GROUPS
    matches = expert_ids[:, :, None] == routed[None, None, :]
    routed_here = jnp.any(matches, axis=1).astype(jnp.int32)
    slot_rank = jnp.cumsum(routed_here, axis=0) - routed_here
    slot_hot = jnp.logical_and(
        slot_rank[:, :, None] == jnp.arange(CAP, dtype=jnp.int32)[None, None, :],
        routed_here[:, :, None] == 1,
    )
    gates = gate_probs.astype(jnp.float32)
    gate_sel = jnp.sum(jnp.where(matches, gates[:, :, None], 0.0), axis=1)
    placer = slot_hot.astype(jnp.bfloat16).reshape(tok_here, columns * CAP)
    placer_gate = (
        jnp.where(slot_hot, gate_sel[:, :, None], 0.0).astype(jnp.bfloat16).reshape(tok_here, columns * CAP)
    )
    width = w_gate.shape[2]

    def tiles_of(place, source, at, size):
        tiles = lax.dot_general(
            place, source[:, at : at + size], (((0,), (0,)), ((), ())), preferred_element_type=jnp.float32
        )
        return tiles.astype(jnp.bfloat16).reshape(columns, CAP, size)

    def on(block, *ties):
        return hop(after(block, *ties), 1)

    def back(block, *ties):
        return hop(after(block, *ties), -1)

    def swap(part):
        return shift(part, "core", 1)

    features = tokens.shape[1]
    all_rows = NX * NC * columns * CAP
    split = all_rows * 3 // 4

    raw = tiles_of(placer, tokens, X_REST, X_RAW).reshape(-1, X_RAW)
    on_r, back_r = hop(raw, 1), hop(raw, -1)
    x = exchange_yz(after(tiles_of(placer, tokens, 0, X_REST), raw))
    middle = raw.shape[0] // 2
    again_r = jnp.concatenate([hop(on_r[:middle], 1), hop(back_r[middle:], -1)])
    rounds = [part.reshape(columns, CAP, X_RAW) for part in (raw, on_r, back_r, again_r)]
    dy = tiles_of(placer_gate, cotangent, 0, features)
    rounds = jnp.concatenate(rounds, axis=2)

    ties = (x, rounds, dy, row_order())
    order = lax.optimization_barrier(ties)[3]
    on_x, back_x = on(x, *ties), back(x, *ties)
    other_x, other_on = swap(after(x, *ties)), swap(on_x)
    dy = exchange_yz(after(dy, *ties))

    ties = (dy, on_x, back_x, other_x, other_on)
    again_x, on_dy, back_dy = on(on_x, *ties), on(dy, *ties), back(dy, *ties)
    rounds = exchange_yz(after(rounds, *ties))
    near_x = lax.optimization_barrier((x, on_x, back_x, *ties))[:3]
    near_x = (*near_x, other_x, other_on, swap(near_x[2]))
    other_dy = swap(after(dy, *ties))
    pre = forward(near_x, w_gate, w_up, 0, all_rows)

    ties = (rounds, again_x, on_dy, back_dy, other_dy, pre)
    again_dy = on(on_dy, *ties)
    again_x = (after(again_x, *ties), swap(after(again_x, *ties)))
    rounds = after(rounds, *ties)
    rounds = (rounds, swap(rounds))
    raw_rows = [(part, k * X_RAW, X_RAW) for ks in ((0, 1, 2), (3,)) for part in rounds for k in ks]
    near_dy = lax.optimization_barrier((dy, on_dy, back_dy, *ties))[:3]
    near_dy = (*near_dy, other_dy, swap(near_dy[1]), swap(near_dy[2]))
    pre = forward(again_x, w_gate, w_up, 0, all_rows, split, pre)
    activated, slope, hidden, turned = forward_end(raw_rows, w_gate, w_up, X_REST, pre)

    known = project(near_dy[:4], w_down)

    ties = (again_dy, *near_dy, turned, known)
    again_dy = (again_dy, swap(after(again_dy, *ties)))
    grad_down, grad_pre_gate, grad_pre_up, row_gate = down_terms(
        (*near_dy, *again_dy), w_down, turned, known, activated, slope, hidden, order
    )
    returned = return_rows(row_gate).reshape(columns, CAP)
    grads = up_terms((*near_x, *again_x), raw_rows, grad_pre_gate, grad_pre_up)

    slot_values = jnp.sum(jnp.where(slot_hot, returned[None], 0.0), axis=2)
    picked = jnp.sum(jnp.where(matches, slot_values[:, None, :], 0.0), axis=2)
    gate_grad = picked / gates
    return *grads, grad_down, gate_grad


def solution(mesh):
    mesh = Mesh(mesh.devices.reshape(NX, NC, NZ, NY), ("x", "core", "z", "y"))
    tokens = P(("x", "core", "z", "y"), None)
    wide = P(("z", "y"), None, ("x", "core"))
    deep = P(("z", "y"), ("x", "core"), None)
    return jax.shard_map(
        per_device,
        mesh=mesh,
        in_specs=(tokens, tokens, tokens, tokens, wide, wide, deep),
        out_specs=(wide, wide, deep, tokens),
        check_vma=False,
    )
```

```python
import math

import jax
import jax.numpy as jnp
from jax import lax
from jax.experimental import pallas as pl
from jax.experimental.pallas import tpu as pltpu
from jax.sharding import Mesh, PartitionSpec as P

GROUPS = 8
CAP = 8
GROUP_SIZE = 32
NX, NC, NZ, NY = 4, 2, 4, 4

X_RAW, X_REST = 1792, 5376
BLOCK, END_BLOCK = 1792, 1792
PARAMS = pltpu.CompilerParams(vmem_limit_bytes=63 * 2**20)


def after(x, *others):
    return x if not others else lax.optimization_barrier((x, *others))[0]


def shift(x, axis, by):
    n = lax.axis_size(axis)
    return lax.ppermute(x, axis, [(i, (i + by) % n) for i in range(n)])


def exchange_yz(tiles):
    return lax.all_to_all(tiles, ("z", "y"), 0, 0, tiled=True).reshape(-1, tiles.shape[2])


def hop(x, by):
    pairs = [(i * NC + c, (i + by * (1 - 2 * c)) % NX * NC + c) for i in range(NX) for c in range(NC)]
    return lax.ppermute(x, ("x", "core"), pairs)


SMALL = pl.CostEstimate(flops=1, bytes_accessed=1, transcendentals=0)
ANY = pl.BlockSpec(memory_space=pl.ANY)


def whole_parts(parts):
    return [part if isinstance(part, tuple) else (part, 0, part.shape[1]) for part in parts]


def row_specs(parts, block, step=lambda i: i):
    return [
        pl.BlockSpec((part.shape[0], block), lambda i, first=at // block: (0, first + step(i))) for part, at, _ in parts
    ]


def joined(refs):
    return jnp.concatenate([ref[...] for ref in refs])


def forward(parts, w_gate, w_up, at, all_rows, row=0, pre=None):
    parts = whole_parts(parts)
    size, count = parts[0][2], len(parts)
    rows = sum(part.shape[0] for part, _, _ in parts)
    width = w_gate.shape[2]
    block = math.gcd(BLOCK, size, at)
    first = at // block

    def kernel(*refs):
        out_ref = refs[-1]

        @pl.when(pl.program_id(0) == 0)
        def _():
            out_ref[...] = jnp.zeros_like(out_ref)

        x = joined(refs[2 : 2 + count])
        for j, w_ref in enumerate(refs[:2]):
            out_ref[:, j * width : (j + 1) * width] += jnp.dot(x, w_ref[0], preferred_element_type=jnp.float32)

    return pl.pallas_call(
        kernel,
        grid=(size // block,),
        in_specs=[pl.BlockSpec((1, block, width), lambda i: (0, first + i, 0))] * 2
        + row_specs(parts, block)
        + ([] if pre is None else [ANY]),
        out_specs=pl.BlockSpec((rows, 2 * width), lambda i: (row // rows, 0)),
        out_shape=jax.ShapeDtypeStruct((all_rows, 2 * width), jnp.float32),
        input_output_aliases={} if pre is None else {2 + count: 0},
        compiler_params=PARAMS,
        cost_estimate=SMALL,
    )(w_gate, w_up, *[part[0] for part in parts], *(() if pre is None else (pre,)))


def forward_end(parts, w_gate, w_up, at, pre):
    parts = whole_parts(parts)
    size, count = parts[0][2], len(parts)
    rows = pre.shape[0]
    width = w_gate.shape[2]
    block = math.gcd(END_BLOCK, size, at)
    first, steps = at // block, size // block
    strip = 128

    def kernel(*refs):
        pre_ref = refs[2 + count]
        activated_ref, slope_ref, hidden_ref, turned_ref, total = refs[-5:]

        @pl.when(pl.program_id(0) == 0)
        def _():
            total[...] = pre_ref[...]

        x = joined(refs[2 : 2 + count])
        for j, w_ref in enumerate(refs[:2]):
            total[:, j * width : (j + 1) * width] += jnp.dot(x, w_ref[0], preferred_element_type=jnp.float32)

        @pl.when(pl.program_id(0) == steps - 1)
        def _():
            for k in range(0, rows, strip):
                place = slice(k, k + strip)
                pre_gate, pre_up = total[place, :width], total[place, width:]
                sig = jax.nn.sigmoid(pre_gate)
                activated = pre_gate * sig
                hidden = (activated * pre_up).astype(jnp.bfloat16)
                activated_ref[place] = activated
                slope_ref[place] = pre_up * sig * (1.0 + pre_gate * (1.0 - sig))
                hidden_ref[place] = hidden
                turned_ref[:, place] = hidden.T

    def whole(*shape):
        return pl.BlockSpec(shape, lambda i: (0, 0))

    flat = jax.ShapeDtypeStruct((rows, width), jnp.float32)
    return pl.pallas_call(
        kernel,
        grid=(steps,),
        in_specs=[pl.BlockSpec((1, block, width), lambda i: (0, first + i, 0))] * 2
        + row_specs(parts, block)
        + [whole(*pre.shape)],
        out_specs=[whole(rows, width)] * 3 + [whole(width, rows)],
        out_shape=[
            flat,
            flat,
            jax.ShapeDtypeStruct((rows, width), jnp.bfloat16),
            jax.ShapeDtypeStruct((width, rows), jnp.bfloat16),
        ],
        scratch_shapes=[pltpu.VMEM(pre.shape, jnp.float32)],
        compiler_params=PARAMS,
        cost_estimate=SMALL,
    )(w_gate, w_up, *[part[0] for part in parts], pre)


def project(parts, w_down):
    parts = whole_parts(parts)
    size = parts[0][2]
    rows, width = sum(part.shape[0] for part, _, _ in parts), w_down.shape[1]
    block = math.gcd(BLOCK, size)

    def kernel(down_ref, *refs):
        out_ref = refs[-1]

        @pl.when(pl.program_id(0) == 0)
        def _():
            out_ref[...] = jnp.zeros_like(out_ref)

        out_ref[...] += lax.dot_general(
            joined(refs[:-1]), down_ref[0], (((1,), (1,)), ((), ())), preferred_element_type=jnp.float32
        )

    return pl.pallas_call(
        kernel,
        grid=(size // block,),
        in_specs=[pl.BlockSpec((1, width, block), lambda i: (0, 0, i))] + row_specs(parts, block),
        out_specs=pl.BlockSpec((rows, width), lambda i: (0, 0)),
        out_shape=jax.ShapeDtypeStruct((rows, width), jnp.float32),
        compiler_params=PARAMS,
        cost_estimate=SMALL,
    )(w_down, *[part[0] for part in parts])


def down_terms(parts, w_down, turned, projected, activated, slope, hidden, order):
    parts = whole_parts(parts)
    size, count = parts[0][2], len(parts)
    rows, width = hidden.shape
    block = math.gcd(BLOCK, size)
    steps = size // block
    strip, known = rows // (NX * NC), projected.shape[0]
    late = (activated, slope, hidden, projected)
    n_late = len(late)

    def kernel(*refs):
        order_ref, down_ref, turned_ref = refs[:3]
        late_refs = refs[3 : 3 + n_late]
        grad_ref, gate_ref, up_ref, row_ref, projected_ref = refs[-6 - n_late : -1 - n_late]
        held, sems = refs[-1 - n_late : -1], refs[-1]
        copies = [pltpu.make_async_copy(late, own, sems.at[k]) for k, (late, own) in enumerate(zip(late_refs, held))]

        @pl.when(pl.program_id(0) == 0)
        def _():
            for copy in copies:
                copy.start()
            projected_ref[known:] = jnp.zeros_like(projected_ref[known:])

        dy = joined(refs[3 + n_late : 3 + n_late + count])
        projected_ref[known:] += lax.dot_general(
            dy[known:], down_ref[0], (((1,), (1,)), ((), ())), preferred_element_type=jnp.float32
        )
        grad_ref[0] = jnp.dot(turned_ref[...], dy, preferred_element_type=jnp.float32).astype(jnp.bfloat16)

        @pl.when(pl.program_id(0) == steps - 1)
        def _():
            for copy in copies:
                copy.wait()
            activated_ref, slope_ref, hidden_ref, known_ref = held
            projected_ref[:known] = known_ref[...]
            row = lax.broadcasted_iota(jnp.int32, (strip // CAP, strip), 1)
            source = lax.broadcasted_iota(jnp.int32, (strip // CAP, strip), 0)
            of_source = (row // CAP == source).astype(jnp.float32)
            row = lax.broadcasted_iota(jnp.int32, (strip, CAP), 0)
            slot = lax.broadcasted_iota(jnp.int32, (strip, CAP), 1)
            in_slot = row % CAP == slot

            for k in range(rows // strip):
                at_rows = slice(k * strip, (k + 1) * strip)
                projected = projected_ref[at_rows]
                gate_ref[at_rows] = (projected * slope_ref[at_rows]).astype(jnp.bfloat16)
                up_ref[at_rows] = (projected * activated_ref[at_rows]).astype(jnp.bfloat16)
                sums = jnp.sum(hidden_ref[at_rows].astype(jnp.float32) * projected, axis=1, keepdims=True)
                place = pl.ds(pl.multiple_of(order_ref[k] * (strip // CAP), strip // CAP), strip // CAP)
                row_ref[place] = jnp.dot(
                    of_source, jnp.where(in_slot, sums, 0.0), precision=lax.Precision.HIGHEST
                )

    def whole(*shape):
        return pl.BlockSpec(shape, lambda i: (0, 0))

    wide = pl.BlockSpec((1, width, block), lambda i: (0, 0, i))
    grad = jax.ShapeDtypeStruct((rows, width), jnp.bfloat16)
    return pl.pallas_call(
        kernel,
        grid=(steps,),
        in_specs=[pl.BlockSpec(memory_space=pltpu.SMEM), wide, whole(width, rows)]
        + [ANY] * len(late)
        + row_specs(parts, block),
        out_specs=[wide, whole(rows, width), whole(rows, width), whole(rows // CAP, CAP)],
        out_shape=[
            jax.ShapeDtypeStruct(w_down.shape, jnp.bfloat16),
            grad,
            grad,
            jax.ShapeDtypeStruct((rows // CAP, CAP), jnp.float32),
        ],
        scratch_shapes=[pltpu.VMEM((rows, width), jnp.float32)]
        + [pltpu.VMEM(a.shape, a.dtype) for a in late]
        + [pltpu.SemaphoreType.DMA((len(late),))],
        compiler_params=PARAMS,
        cost_estimate=SMALL,
    )(order, w_down, turned, *late, *[part[0] for part in parts])


def up_terms(parts, last_parts, grad_pre_gate, grad_pre_up):
    rows, width = grad_pre_gate.shape
    parts, last_parts = whole_parts(parts), whole_parts(last_parts)
    count, size, last = len(parts), parts[0][2], last_parts[0][2]
    block = math.gcd(BLOCK, size, last)
    steps, last_steps = size // block, last // block

    def kernel(*refs):
        out_refs = refs[-2:]

        def write(row_refs):
            x = joined(row_refs)
            pre = jnp.concatenate([ref[...] for ref in refs[:2]], axis=1)
            both = lax.dot_general(x, pre, (((0,), (0,)), ((), ())), preferred_element_type=jnp.float32)
            for k, out_ref in enumerate(out_refs):
                out_ref[0] = both[:, k * width : (k + 1) * width].astype(jnp.bfloat16)

        pl.when(pl.program_id(0) < steps)(lambda: write(refs[2 : 2 + count]))
        pl.when(pl.program_id(0) >= steps)(lambda: write(refs[2 + count : -2]))

    out = jax.ShapeDtypeStruct((1, size + last, width), jnp.bfloat16)
    whole = pl.BlockSpec((rows, width), lambda i: (0, 0))
    return pl.pallas_call(
        kernel,
        grid=(steps + last_steps,),
        in_specs=[whole, whole]
        + row_specs(parts, block, lambda i: jnp.minimum(i, steps - 1))
        + row_specs(last_parts, block, lambda i: jnp.maximum(i - steps, 0)),
        out_specs=[pl.BlockSpec((1, block, width), lambda i: (0, i, 0))] * 2,
        out_shape=[out, out],
        compiler_params=PARAMS,
        cost_estimate=SMALL,
    )(grad_pre_gate, grad_pre_up, *[part[0] for part in (*parts, *last_parts)])


def row_order():
    x, core = lax.axis_index("x"), lax.axis_index("core")
    near = [(c, by) for c in (core, 1 - core) for by in (0, 1, -1)]
    return jnp.stack([(x - by * (1 - 2 * c)) % NX * NC + c for c, by in near + [(core, 2), (1 - core, 2)]]).astype(jnp.int32)


def return_rows(row_gate):
    got = lax.all_to_all(row_gate, ("x", "core", "z", "y"), 0, 0, tiled=True)
    return jnp.sum(got.reshape(NC * NX, NZ * NY, CAP), axis=0)


def per_device(tokens, cotangent, expert_ids, gate_probs, w_gate, w_up, w_down):
    tok_here = tokens.shape[0]
    columns = NZ * NY
    experts = jnp.arange(columns, dtype=jnp.int32)
    routed = experts % GROUPS * GROUP_SIZE + experts // GROUPS
    matches = expert_ids[:, :, None] == routed[None, None, :]
    routed_here = jnp.any(matches, axis=1).astype(jnp.int32)
    slot_rank = jnp.cumsum(routed_here, axis=0) - routed_here
    slot_hot = jnp.logical_and(
        slot_rank[:, :, None] == jnp.arange(CAP, dtype=jnp.int32)[None, None, :],
        routed_here[:, :, None] == 1,
    )
    gates = gate_probs.astype(jnp.float32)
    gate_sel = jnp.sum(jnp.where(matches, gates[:, :, None], 0.0), axis=1)
    placer = slot_hot.astype(jnp.bfloat16).reshape(tok_here, columns * CAP)
    placer_gate = (
        jnp.where(slot_hot, gate_sel[:, :, None], 0.0).astype(jnp.bfloat16).reshape(tok_here, columns * CAP)
    )
    width = w_gate.shape[2]

    def tiles_of(place, source, at, size):
        tiles = lax.dot_general(
            place, source[:, at : at + size], (((0,), (0,)), ((), ())), preferred_element_type=jnp.float32
        )
        return tiles.astype(jnp.bfloat16).reshape(columns, CAP, size)

    def on(block, *ties):
        return hop(after(block, *ties), 1)

    def back(block, *ties):
        return hop(after(block, *ties), -1)

    def swap(part):
        return shift(part, "core", 1)

    features = tokens.shape[1]
    all_rows = NX * NC * columns * CAP
    split = all_rows * 3 // 4

    raw = tiles_of(placer, tokens, X_REST, X_RAW).reshape(-1, X_RAW)
    on_r, back_r = hop(raw, 1), hop(raw, -1)
    x = exchange_yz(after(tiles_of(placer, tokens, 0, X_REST), raw))
    middle = raw.shape[0] // 2
    again_r = jnp.concatenate([hop(on_r[:middle], 1), hop(back_r[middle:], -1)])
    rounds = [part.reshape(columns, CAP, X_RAW) for part in (raw, on_r, back_r, again_r)]
    dy = tiles_of(placer_gate, cotangent, 0, features)
    rounds = jnp.concatenate(rounds, axis=2)

    ties = (x, rounds, dy, row_order())
    order = lax.optimization_barrier(ties)[3]
    on_x, back_x = on(x, *ties), back(x, *ties)
    other_x, other_on = swap(after(x, *ties)), swap(on_x)
    dy = exchange_yz(after(dy, *ties))

    ties = (dy, on_x, back_x, other_x, other_on)
    again_x, on_dy, back_dy = on(on_x, *ties), on(dy, *ties), back(dy, *ties)
    rounds = exchange_yz(after(rounds, *ties))
    near_x = lax.optimization_barrier((x, on_x, back_x, *ties))[:3]
    near_x = (*near_x, other_x, other_on, swap(near_x[2]))
    other_dy = swap(after(dy, *ties))
    pre = forward(near_x, w_gate, w_up, 0, all_rows)

    ties = (rounds, again_x, on_dy, back_dy, other_dy, pre)
    again_dy = on(on_dy, *ties)
    again_x = (after(again_x, *ties), swap(after(again_x, *ties)))
    rounds = after(rounds, *ties)
    rounds = (rounds, swap(rounds))
    raw_rows = [(part, k * X_RAW, X_RAW) for ks in ((0, 1, 2), (3,)) for part in rounds for k in ks]
    near_dy = lax.optimization_barrier((dy, on_dy, back_dy, *ties))[:3]
    near_dy = (*near_dy, other_dy, swap(near_dy[1]), swap(near_dy[2]))
    pre = forward(again_x, w_gate, w_up, 0, all_rows, split, pre)
    activated, slope, hidden, turned = forward_end(raw_rows, w_gate, w_up, X_REST, pre)

    known = project(near_dy[:4], w_down)

    ties = (again_dy, *near_dy, turned, known)
    again_dy = (again_dy, swap(after(again_dy, *ties)))
    grad_down, grad_pre_gate, grad_pre_up, row_gate = down_terms(
        (*near_dy, *again_dy), w_down, turned, known, activated, slope, hidden, order
    )
    returned = return_rows(row_gate).reshape(columns, CAP)
    grads = up_terms((*near_x, *again_x), raw_rows, grad_pre_gate, grad_pre_up)

    slot_values = jnp.sum(jnp.where(slot_hot, returned[None], 0.0), axis=2)
    picked = jnp.sum(jnp.where(matches, slot_values[:, None, :], 0.0), axis=2)
    gate_grad = picked / gates
    return *grads, grad_down, gate_grad


def solution(mesh):
    mesh = Mesh(mesh.devices.reshape(NX, NC, NZ, NY), ("x", "core", "z", "y"))
    tokens = P(("x", "core", "z", "y"), None)
    wide = P(("z", "y"), None, ("x", "core"))
    deep = P(("z", "y"), ("x", "core"), None)
    return jax.shard_map(
        per_device,
        mesh=mesh,
        in_specs=(tokens, tokens, tokens, tokens, wide, wide, deep),
        out_specs=(wide, wide, deep, tokens),
        check_vma=False,
    )
```
